128 devices in a mesh: region: 16 (over y, z), sub: 8 (over x, core).
Axes of the slice: x: 4, y: 4, z: 4, core: 2. Of those that a mesh axis runs over, the one named last changes fastest.
Arguments:
- right_side: float32 [3, 131072], P(None, ('region', 'sub')), may hold values from -6 to 6
- node_mass: float32 [131072], P(('region', 'sub')), may hold values from 0.5 to 2
- precond: float32 [9, 131072], P(None, ('region', 'sub')), as said below
- elem_hess: float32 [144, 524288], P(None, ('region', 'sub')), as said below
- elem_nodes: int32 [4, 524288], P(None, ('region', 'sub')), may hold values from 0 to 1151, as said below
- halo_lists: int32 [2, 8192], P(None, ('region', 'sub')), may hold values from 0 to 1023
- contact_hess: float32 [144, 262144], P(None, ('region', 'sub')), as said below
- pair_point: int32 [262144], P(('region', 'sub')), may hold values from 0 to 1023
- pair_slot: int32 [3, 262144], P(None, ('region', 'sub')), may hold values from 0 to 1535, as said below
- pair_live: int32 [262144], P(('region', 'sub')), may hold values from 0 to 1, as said below
- contact_send: int32 [128, 12, 128], P(('region', 'sub')), may hold values from 0 to 1023
- send_counts: int32 [128, 12], P(('region', 'sub')), may hold values from 32 to 128, as said below
Outputs:
- solution: float32 [3, 131072], P(None, ('region', 'sub'))
- residual: float32 [3, 131072], P(None, ('region', 'sub'))
The draws below stay inside these ranges and needn't reach their ends.
Inputs may be any that keep to these rules, and one draw needn't show every extreme that they name: `elem_nodes`: on part p, ids below 1024 are own vertices, ids from 1024 to 1087 name the lower neighbour's upward list, higher ids the upper neighbour's downward list; the first part never uses the lower block and the last part never the upper block. `send_counts`: entry [q, k] counts the live entries at the front of list k of part q. In every draw some part receives 128 live entries from each of its partners other than itself; the list that a part keeps for itself (k = 0) holds at most 64. `pair_slot`: slot s = k * 128 + i names entry i of list k of part (p - o_k) mod 128, for the pair's part p. Row 0 always names a live entry; rows 1 and 2 may name dead entries, and then only in the list that part p keeps for itself (k = 0); row 1 names a dead entry only where row 2 does. `pair_live`: between 512 and 2048 pair slots of each part are live; on some part all are. `elem_hess`: every 12x12 block is symmetric positive definite. `contact_hess`: every 12x12 block is symmetric positive definite. `precond`: every 3x3 block is symmetric positive definite.
All inputs are finite; a program needn't handle non-finite values.
Results may differ from the reference program's by a relative error of at most 0.00011.
Values sent between devices are 32-bit elements; how exact they have to be, the bound alone decides.
A program may use at most 128 MiB of HBM per device.

```python
import math
import jax
import jax.numpy as jnp

NODE_DEV = 1024
ITERS = 2
PEERS = 12
ELEM_DEV = 4096
PAIRS_DEV = 2048
HALO = 64
CAP = 128
NODES = 131072
ELEMS = 524288
PAIRS = 262144
DEVICES = 128


def definite_blocks(key, count, shrink):
    first, second = jax.random.split(key)
    factor = jax.random.normal(first, (12, 12, count), jnp.float32)
    blocks = jnp.einsum('ike,jke->ije', factor, factor) / 12.0 + 0.5 * jnp.eye(12, dtype=jnp.float32)[:, :, None]
    stiffness = jnp.exp(jax.random.uniform(second, (count,), jnp.float32, -1.2039728, 1.0986123))
    return (blocks * (stiffness * shrink)[None, None, :]).reshape(144, count)


def draw_elem_hess(key, part):
    return definite_blocks(jax.random.fold_in(key, 1), ELEMS, NODE_DEV / (4.0 * ELEM_DEV))


def draw_contact_hess(key, part):
    return definite_blocks(jax.random.fold_in(key, 2), PAIRS, NODE_DEV / (8.0 * PAIRS_DEV))


def draw_precond(key, part):
    first, second = jax.random.split(jax.random.fold_in(key, 3))
    factor = jax.random.normal(first, (3, 3, NODES), jnp.float32)
    blocks = jnp.einsum('ike,jke->ije', factor, factor) / 3.0 + 0.5 * jnp.eye(3, dtype=jnp.float32)[:, :, None]
    scales = 0.3 * jnp.exp(jax.random.uniform(second, (NODES,), jnp.float32, -0.6931472, 0.6931472))
    return (blocks * scales[None, None, :]).reshape(9, NODES)


def draw_elem_nodes(key, part):
    raw_ids = jax.random.randint(jax.random.fold_in(key, 4), (4, DEVICES, ELEM_DEV), 0, NODE_DEV + 2 * HALO)
    device_ids = jnp.arange(DEVICES, dtype=jnp.int32)[None, :, None]
    in_lower = (raw_ids >= NODE_DEV) & (raw_ids < NODE_DEV + HALO) & (device_ids == 0)
    in_upper = (raw_ids >= NODE_DEV + HALO) & (device_ids == DEVICES - 1)
    fixed_ids = jnp.where(in_lower, raw_ids - NODE_DEV, raw_ids)
    fixed_ids = jnp.where(in_upper, raw_ids - NODE_DEV - HALO, fixed_ids)
    return fixed_ids.reshape(4, ELEMS).astype(jnp.int32)


def partner_shifts_drawn():
    middle = DEVICES // 2
    return jnp.array([0, 1, 2, 3, 4, -1, -2, -3, -4, middle, middle + 1, middle - 1], dtype=jnp.int32)


def contact_plan(key):
    first, second, third = jax.random.split(jax.random.fold_in(key, 7), 3)
    counts = jax.random.randint(first, (DEVICES, PEERS), CAP // 4, 3 * CAP // 4 + 1)
    self_counts = jax.random.randint(third, (DEVICES, 1), CAP // 4, CAP // 2 + 1)
    column_ids = jnp.arange(PEERS, dtype=jnp.int32)[None, :]
    counts = jnp.where(column_ids == 0, self_counts, counts)
    busy_part = jax.random.randint(second, (), 0, DEVICES)
    owner_ids = jnp.arange(DEVICES, dtype=jnp.int32)[:, None]
    feeds_busy = ((owner_ids + partner_shifts_drawn()[None, :]) % DEVICES == busy_part) & (column_ids > 0)
    return jnp.where(feeds_busy, CAP, counts).astype(jnp.int32)


def draw_send_counts(key, part):
    return contact_plan(key)


def draw_pair_slot(key, part):
    counts = contact_plan(key)
    part_ids = jnp.arange(DEVICES, dtype=jnp.int32)[:, None]
    owner_ids = (part_ids - partner_shifts_drawn()[None, :]) % DEVICES
    incoming = counts[owner_ids, jnp.arange(PEERS, dtype=jnp.int32)[None, :]]
    upper_ends = jnp.cumsum(incoming, axis=1).astype(jnp.int32)
    starts = upper_ends - incoming
    totals = upper_ends[:, -1]
    drawn_rows = jax.random.randint(jax.random.fold_in(key, 11), (DEVICES, 3 * PAIRS_DEV), 0, totals[:, None])
    partner_index = jax.vmap(lambda e, p: jnp.searchsorted(e, p, side='right'))(upper_ends, drawn_rows).astype(jnp.int32)
    entry_index = drawn_rows - jnp.take_along_axis(starts, partner_index, axis=1)
    live_slot = (partner_index * CAP + entry_index).reshape(DEVICES, 3, PAIRS_DEV)
    pair_kind = jax.random.randint(jax.random.fold_in(key, 19), (DEVICES, 1, PAIRS_DEV), 0, 20)
    row_ids = jnp.arange(3, dtype=jnp.int32)[None, :, None]
    unused = (row_ids == 2) & (pair_kind >= 10) | (row_ids == 1) & (pair_kind >= 17)
    dead_slot = jax.random.randint(jax.random.fold_in(key, 23), (DEVICES, 3, PAIRS_DEV), counts[:, 0][:, None, None], CAP)
    slot_index = jnp.where(unused, dead_slot, live_slot)
    return jnp.transpose(slot_index, (1, 0, 2)).reshape(3, PAIRS).astype(jnp.int32)


def draw_pair_live(key, part):
    first, second = jax.random.split(jax.random.fold_in(key, 13))
    live_count = jax.random.randint(first, (DEVICES,), PAIRS_DEV // 4, PAIRS_DEV + 1)
    full_part = jax.random.randint(second, (), 0, DEVICES)
    live_count = jnp.where(jnp.arange(DEVICES, dtype=jnp.int32) == full_part, PAIRS_DEV, live_count)
    part_keys = jax.random.split(jax.random.fold_in(key, 17), DEVICES)
    ranks = jax.vmap(lambda k: jax.random.permutation(k, PAIRS_DEV))(part_keys)
    return (ranks < live_count[:, None]).astype(jnp.int32).reshape(PAIRS)


def place_ends(drawn, stream_key, low, high):
    dims = drawn.shape
    place = [jax.random.randint(jax.random.fold_in(stream_key, axis), (), 0, dims[axis]) for axis in range(len(dims))]
    drawn = drawn.at[tuple(place)].set(low)
    longest = dims.index(max(dims))
    place[longest] = (place[longest] + 1) % dims[longest]
    return drawn.at[tuple(place)].set(high)


def steps_of(rng, dims, cuts, smallest, high):
    def one(position, blocks):
        heights = jax.random.uniform(jax.random.fold_in(jax.random.fold_in(rng, 6), position), (blocks,), jnp.float32, smallest / len(cuts), high / len(cuts))
        return jnp.repeat(jnp.exp(heights), dims[position] // blocks).reshape((-1,) + (1,) * (len(dims) - position - 1))

    level = one(*cuts[0])
    for cut in cuts[1:]:
        level = level * one(*cut)
    return level


def gaussian(own_key, shape, spread, bound, cuts=(), held_as=jnp.bfloat16):
    gain = steps_of(own_key, shape, cuts, -0.22, 0.18) if cuts else 1.0
    values = jax.random.normal(own_key, shape, jnp.float32) * spread * gain
    return jnp.minimum(jnp.maximum(values, -bound), bound).astype(held_as)


def setup_inputs(seed: int = 0) -> dict:
    arg_keys = jax.random.split(jax.random.key(seed), 13)
    return {
        "right_side": gaussian(arg_keys[0], (3, NODES), 1.0, 6.0, ((1, 128),), jnp.float32),
        "node_mass": jnp.clip(jnp.exp(math.log(2.0) - 1.3862944 * jax.random.uniform(arg_keys[1], (NODES,), jnp.float32) ** steps_of(arg_keys[1], (NODES,), ((0, 128),), -0.2, 0.2)), 0.5, 2.0),
        "precond": draw_precond(jax.random.fold_in(arg_keys[12], 71), 0),
        "elem_hess": draw_elem_hess(jax.random.fold_in(arg_keys[12], 71), 0),
        "elem_nodes": draw_elem_nodes(jax.random.fold_in(arg_keys[12], 71), 0),
        "halo_lists": place_ends(jax.random.randint(arg_keys[5], (2, HALO * DEVICES), 0, NODE_DEV), jax.random.fold_in(arg_keys[5], 1), 0, NODE_DEV - 1).astype(jnp.int32),
        "contact_hess": draw_contact_hess(jax.random.fold_in(arg_keys[12], 71), 0),
        "pair_point": place_ends(jax.random.randint(arg_keys[7], (PAIRS,), 0, NODE_DEV), jax.random.fold_in(arg_keys[7], 1), 0, NODE_DEV - 1).astype(jnp.int32),
        "pair_slot": draw_pair_slot(jax.random.fold_in(arg_keys[12], 71), 0),
        "pair_live": draw_pair_live(jax.random.fold_in(arg_keys[12], 71), 0),
        "contact_send": place_ends(jax.random.randint(arg_keys[10], (DEVICES, PEERS, CAP), 0, NODE_DEV), jax.random.fold_in(arg_keys[10], 1), 0, NODE_DEV - 1).astype(jnp.int32),
        "send_counts": draw_send_counts(jax.random.fold_in(arg_keys[12], 71), 0),
    }


def partner_shifts():
    middle = DEVICES // 2
    return jnp.array([0, 1, 2, 3, 4, -1, -2, -3, -4, middle, middle + 1, middle - 1], dtype=jnp.int32)


def element_ids(elem_nodes, halo_lists):
    local_ids = elem_nodes.reshape(4, DEVICES, ELEM_DEV)
    halo_table = halo_lists.reshape(2, DEVICES, HALO)
    device_ids = jnp.arange(DEVICES, dtype=jnp.int32)[None, :, None]
    lower_part = jnp.clip(device_ids - 1, 0, DEVICES - 1)
    upper_part = jnp.clip(device_ids + 1, 0, DEVICES - 1)
    low_slot = jnp.clip(local_ids - NODE_DEV, 0, HALO - 1)
    high_slot = jnp.clip(local_ids - NODE_DEV - HALO, 0, HALO - 1)
    own_id = device_ids * NODE_DEV + local_ids
    low_id = lower_part * NODE_DEV + halo_table[1][lower_part, low_slot]
    high_id = upper_part * NODE_DEV + halo_table[0][upper_part, high_slot]
    global_ids = jnp.where(local_ids < NODE_DEV, own_id, jnp.where(local_ids < NODE_DEV + HALO, low_id, high_id))
    return global_ids.reshape(4, ELEMS).astype(jnp.int32)


def contact_ids(pair_point, pair_slot, contact_send, send_counts):
    device_ids = jnp.arange(DEVICES, dtype=jnp.int32)[None, :, None]
    slot_index = pair_slot.reshape(3, DEVICES, PAIRS_DEV)
    partner_index = (slot_index // CAP).astype(jnp.int32)
    entry_index = (slot_index % CAP).astype(jnp.int32)
    owner_part = ((device_ids - partner_shifts()[partner_index]) % DEVICES).astype(jnp.int32)
    tri_id = owner_part * NODE_DEV + contact_send[owner_part, partner_index, entry_index]
    tri_weight = (entry_index < send_counts[owner_part, partner_index]).astype(jnp.float32)
    point_id = (device_ids[0] * NODE_DEV + pair_point.reshape(DEVICES, PAIRS_DEV))[None]
    global_ids = jnp.concatenate([point_id, tri_id], axis=0).reshape(4, PAIRS).astype(jnp.int32)
    weights = jnp.concatenate([jnp.ones_like(tri_weight[:1]), tri_weight], axis=0).reshape(4, PAIRS)
    return global_ids, weights


def block_apply(hessian, global_ids, weights, gate, vector):
    gathered = vector[:, global_ids] * weights[None]
    stacked = jnp.transpose(gathered, (1, 0, 2)).reshape(12, -1)
    blocks = hessian.reshape(12, 12, -1)
    product = jnp.zeros_like(stacked)
    for column in range(12):
        product = product + blocks[:, column, :] * stacked[column][None, :]
    product = product * gate[None]
    scattered = jnp.transpose(product.reshape(4, 3, -1), (0, 2, 1)) * weights[:, :, None]
    summed = jax.ops.segment_sum(scattered.reshape(-1, 3), global_ids.reshape(-1), num_segments=NODES)
    return summed.T


def reference(right_side, node_mass, precond, elem_hess, elem_nodes, halo_lists, contact_hess, pair_point, pair_slot, pair_live, contact_send, send_counts):
    elem_id = element_ids(elem_nodes, halo_lists)
    elem_weight = jnp.ones(elem_id.shape, jnp.float32)
    elem_gate = jnp.ones((ELEMS,), jnp.float32)
    pair_id, pair_weight = contact_ids(pair_point, pair_slot, contact_send, send_counts)
    pair_gate = pair_live.astype(jnp.float32)
    pre_blocks = precond.reshape(3, 3, -1)

    def apply_matrix(vector):
        total = node_mass[None] * vector
        total = total + block_apply(elem_hess, elem_id, elem_weight, elem_gate, vector)
        return total + block_apply(contact_hess, pair_id, pair_weight, pair_gate, vector)

    def precondition(residual):
        return jnp.sum(pre_blocks * residual[None], axis=1)

    solution = jnp.zeros_like(right_side)
    residual = right_side
    search = precondition(residual)
    direction = search
    gamma_now = jnp.sum(residual * search)
    for iteration in range(ITERS):
        image_vec = apply_matrix(direction)
        alpha_step = gamma_now / jnp.sum(direction * image_vec)
        solution = solution + alpha_step * direction
        residual = residual - alpha_step * image_vec
        if iteration + 1 < ITERS:
            search = precondition(residual)
            gamma_next = jnp.sum(residual * search)
            direction = search + (gamma_next / gamma_now) * direction
            gamma_now = gamma_next
    return solution, residual
```

```python
import jax
import jax.numpy as jnp
from jax import lax
from jax.experimental import pallas as pl
from jax.experimental.pallas import tpu as pltpu
from jax.sharding import PartitionSpec as P

MESH = pl.DeviceIdType.MESH
AXES = ("region", "sub")
F32 = jnp.float32
BF16 = jnp.bfloat16
LANES = 128
OFFSETS = (0, 1, 2, 3, 4, -1, -2, -3, -4, 64, 65, 63)
PEERS = len(OFFSETS)
UP, DOWN = 1, 5
NODE_BLOCKS = 8
ELEM_CHUNKS = 32
PAIR_CHUNKS = 16
ELEM_ROW, POINT_ROW, SLOT_ROW, LIST_ROW, ID_ROWS = 0, 128, 144, 192, 208
HALO_ROW = PEERS
OWN_ROWS = 80


def spread(row):
    return jnp.broadcast_to(row, (8, LANES))


def pick(tables, ids):
    block, lane = ids >> 7, ids & 127
    found = [jnp.zeros(ids.shape, F32) for _ in range(3)]
    for h in range(len(tables[0])):
        hit = block == h
        for m in range(3):
            value = jnp.take_along_axis(tables[m][h], lane, axis=1, mode="promise_in_bounds")
            found[m] = jnp.where(hit, value, found[m])
    return found


def block_product(hess, start, z, row):
    lanes = pl.ds(start, LANES)
    low = row < 4
    acc0 = acc1 = acc2 = None
    for j in range(6):
        za, zb = z[2 * j], z[2 * j + 1]
        t0 = hess[24 * j : 24 * j + 8, lanes] * za
        t1 = hess[24 * j + 8 : 24 * j + 16, lanes] * jnp.where(low, za, zb)
        t2 = hess[24 * j + 16 : 24 * j + 24, lanes] * zb
        if j == 0:
            acc0, acc1, acc2 = t0, t1, t2
        else:
            acc0, acc1, acc2 = acc0 + t0, acc1 + t1, acc2 + t2
    first = acc0 + pltpu.roll(jnp.where(low, acc2, acc1), 4, 0)
    last = acc1 + pltpu.roll(acc2, 4, 0)
    return first, last


def split(x):
    top = x.astype(BF16).astype(F32)
    return top, x - top


def vertex_rows(first, last, row):
    f0, f1 = split(first)
    l0, l1 = split(last)
    near = row < 3
    a0 = jnp.where(near, f0, pltpu.roll(f1, 3, 0))
    a1 = jnp.where(near, pltpu.roll(f0, 5, 0), f1)
    fl0 = jnp.where(row < 1, l0, f0)
    fl1 = jnp.where(row < 1, l1, f1)
    a2 = jnp.where(near, pltpu.roll(fl0, 2, 0), pltpu.roll(fl1, 5, 0))
    a3 = jnp.where(near, pltpu.roll(l0, 7, 0), pltpu.roll(l1, 2, 0))
    return a0, a1, a2, a3


def place(y8, block, count, rows):
    parts = [jnp.where(block == h, y8, 0.0) for h in range(count)]
    if rows > 8 * count:
        parts.append(jnp.zeros((rows - 8 * count, LANES), F32))
    return jnp.concatenate(parts, axis=0).astype(BF16)


def gather_sum(placed, hot):
    return lax.dot_general(placed, hot, (((1,), (1,)), ((), ())), preferred_element_type=F32)


def kernel(
    right_hbm, mass_hbm, precond_hbm, ehess_hbm, enodes_hbm, halo_hbm, chess_hbm, point_hbm, slot_hbm,
    live_hbm, list_hbm, count_hbm,
    sol_ref, res_ref,
    right, mass, precond, ehess, enodes, halo, chess, point, slot, live, lists, count,
    ids, hot, ztab, own_tab, got_tab, zelem, zpoint, vert, total,
    send_v, recv_v, send_r, recv_r, sum_send, sum_a, sum_b,
    in_sem, sv_sem, rv_sem, sr_sem, rr_sem, ss_sem, ra_sem, rb_sem,
):
    region, sub = lax.axis_index("region"), lax.axis_index("sub")
    part = region * 8 + sub

    def device(offset):
        q = lax.rem(part + offset + 128, 128)
        return (lax.div(q, 8), lax.rem(q, 8))

    def sub_peer(j):
        return (region, lax.rem(sub + j, 8))

    def region_peer(j):
        return (lax.rem(region + j, 16), sub)

    pairs = [
        (right_hbm, right), (precond_hbm, precond), (list_hbm, lists), (count_hbm, count), (halo_hbm, halo),
        (mass_hbm, mass), (enodes_hbm, enodes), (point_hbm, point), (slot_hbm, slot), (live_hbm, live),
        (chess_hbm, chess), (ehess_hbm, ehess),
    ]
    copies = [pltpu.make_async_copy(src, dst, in_sem.at[i]) for i, (src, dst) in enumerate(pairs)]
    for copy in copies:
        copy.start()

    barrier = pltpu.get_barrier_semaphore()
    greeted = [device(o) for o in OFFSETS[1:]] + [sub_peer(j) for j in range(1, 8)]
    greeted += [region_peer(j) for j in range(1, 16) if j != 8]
    for peer in greeted:
        pl.semaphore_signal(barrier, inc=1, device_id=peer, device_id_type=MESH)

    row = lax.broadcasted_iota(jnp.int32, (8, LANES), 0)
    lane = lax.broadcasted_iota(jnp.int32, (8, LANES), 1)

    for copy in copies[:6]:
        copy.wait()
    for m in range(3):
        for j in range(8):
            vert[m, j : j + 1, :] = right[m : m + 1, j * LANES : (j + 1) * LANES]
    for k in range(9):
        for j in range(8):
            vert[3 + k, j : j + 1, :] = precond[k : k + 1, j * LANES : (j + 1) * LANES]

    def precondition(vec):
        return [sum(vert[3 + 3 * m + l] * vec[l] for l in range(3)) for m in range(3)]

    ids[LIST_ROW : LIST_ROW + PEERS, :] = lists[...]
    ids[LIST_ROW + PEERS : LIST_ROW + PEERS + 1, :] = jnp.concatenate([halo[1:2, :], halo[0:1, :]], axis=1)
    ids[LIST_ROW + PEERS + 1 : ID_ROWS, :] = jnp.zeros((ID_ROWS - LIST_ROW - PEERS - 1, LANES), jnp.int32)
    diag = lax.broadcasted_iota(jnp.int32, (16, PEERS), 0) == lax.broadcasted_iota(jnp.int32, (16, PEERS), 1)
    limit = jnp.sum(jnp.where(diag, jnp.broadcast_to(count[...], (16, PEERS)), 0).astype(F32), axis=1, keepdims=True)
    wide_row = lax.broadcasted_iota(jnp.int32, (16, LANES), 0)
    wide_lane = lax.broadcasted_iota(jnp.int32, (16, LANES), 1).astype(F32)
    list_live = jnp.where((wide_lane < limit) | (wide_row == HALO_ROW), 1.0, 0.0)

    def fill_own(vec):
        for m in range(3):
            for h in range(NODE_BLOCKS):
                own_tab[m, h] = spread(vec[m][h : h + 1, :])

    own_tables = [[own_tab.at[m, h] for h in range(NODE_BLOCKS)] for m in range(3)]
    got_tables = [[got_tab.at[m, k] for k in range(PEERS)] for m in range(3)]

    def read(tables):
        return [[t[...] for t in line] for line in tables]

    def offer(turn):
        got = [[], [], []]
        for g in range(2):
            found = pick(read(own_tables), ids[LIST_ROW + 8 * g : LIST_ROW + 8 * g + 8, :])
            for m in range(3):
                got[m].append(found[m] * list_live[8 * g : 8 * g + 8, :])
        for k in range(PEERS):
            for m in range(3):
                send_v[turn, k, m : m + 1, :] = got[m][k // 8][k % 8 : k % 8 + 1, :]
        for k in (UP, DOWN):
            for m in range(3):
                h = HALO_ROW
                send_v[turn, k, 3 + m : 4 + m, :] = got[m][h // 8][h % 8 : h % 8 + 1, :]

    def exchange(src, dst, s_sem, r_sem, turn, sign):
        return [
            pltpu.make_async_remote_copy(
                src_ref=src.at[turn, k], dst_ref=dst.at[turn, k], send_sem=s_sem.at[turn, k],
                recv_sem=r_sem.at[turn, k], device_id=device(sign * OFFSETS[k]), device_id_type=MESH,
            )
            for k in range(1, PEERS)
        ]

    started = []

    def own_lookups():
        def elem_group(g, carry):
            rows = pl.ds(pl.multiple_of(g * 8, 8), 8)
            found = pick(read(own_tables), ids[rows, :])
            for m in range(3):
                zelem[m, rows, :] = found[m]
            return carry

        lax.fori_loop(0, 16, elem_group, 0)
        for g in range(2):
            found = pick(read(own_tables), ids[POINT_ROW + 8 * g : POINT_ROW + 8 * g + 8, :])
            for m in range(3):
                zpoint[m, 8 * g : 8 * g + 8, :] = found[m]

    def halo_lookups(turn):
        for m in range(3):
            ztab[m] = jnp.where(lane < 64, spread(recv_v[turn, UP, 3 + m : 4 + m, :]), spread(recv_v[turn, DOWN, 3 + m : 4 + m, :]))

        def elem_group(g, carry):
            rows = pl.ds(pl.multiple_of(g * 8, 8), 8)
            here = ids[rows, :]
            hit = (here >> 7) == NODE_BLOCKS
            for m in range(3):
                value = jnp.take_along_axis(ztab[m], here & 127, axis=1, mode="promise_in_bounds")
                zelem[m, rows, :] = jnp.where(hit, value, zelem[m, rows, :])
            return carry

        lax.fori_loop(0, 16, elem_group, 0)

    def elements(acc):
        def chunk_group(c, acc):
            for q2 in range(4):
                rows = pl.ds(pl.multiple_of(c * 32 + q2 * 8, 8), 8)
                z8 = [zelem[m, rows, :] for m in range(3)]
                block8 = ids[rows, :] >> 7
                for half in range(2):
                    chunk = c * 8 + q2 * 2 + half
                    start = pl.multiple_of(chunk * LANES, LANES)
                    z = [spread(z8[m][half * 4 + a : half * 4 + a + 1, :]) for a in range(4) for m in range(3)]
                    first, last = block_product(ehess, start, z, row)
                    ys = vertex_rows(first, last, row)
                    placed = jnp.concatenate(
                        [
                            place(ys[a], spread(block8[half * 4 + a : half * 4 + a + 1, :]), 9, OWN_ROWS)
                            for a in range(4)
                        ],
                        axis=1,
                    )
                    k0 = pl.multiple_of(chunk * 4 * LANES, 4 * LANES)
                    acc = acc + gather_sum(placed, hot[:, pl.ds(k0, 4 * LANES)])
            return acc

        return lax.fori_loop(0, ELEM_CHUNKS // 8, chunk_group, acc)

    def contacts(turn, acc):
        for k in range(PEERS):
            for m in range(3):
                got_tab[m, k] = spread(recv_v[turn, k, m : m + 1, :])

        def chunk_group(c, carry):
            acc, acc_slot = carry
            rows = pl.ds(pl.multiple_of(c * 8, 8), 8)
            zp = [zpoint[m, rows, :] for m in range(3)]
            point_block = ids[pl.ds(pl.multiple_of(POINT_ROW + c * 8, 8), 8), :] >> 7
            alive = live[rows, :].astype(F32)
            slot_ids = [ids[pl.ds(pl.multiple_of(SLOT_ROW + c * 24 + 8 * i, 8), 8), :] for i in range(3)]
            zs = [pick(read(got_tables), slot_ids[i]) for i in range(3)]
            slot_block = [s >> 7 for s in slot_ids]
            for q in range(8):
                chunk = c * 8 + q
                start = pl.multiple_of(chunk * LANES, LANES)
                z = [spread(zp[m][q : q + 1, :]) for m in range(3)]
                where = [(3 * q + a) for a in range(3)]
                z += [spread(zs[w // 8][m][w % 8 : w % 8 + 1, :]) for w in where for m in range(3)]
                first, last = block_product(chess, start, z, row)
                gate = spread(alive[q : q + 1, :])
                ys = vertex_rows(first * gate, last * gate, row)
                placed = place(ys[0], spread(point_block[q : q + 1, :]), 8, OWN_ROWS)
                k0 = pl.multiple_of((POINT_ROW + chunk) * LANES, LANES)
                acc = acc + gather_sum(placed, hot[:, pl.ds(k0, LANES)])
                placed = jnp.concatenate(
                    [
                        place(ys[1 + a], spread(slot_block[w // 8][w % 8 : w % 8 + 1, :]), PEERS, 8 * PEERS)
                        for a, w in enumerate(where)
                    ],
                    axis=1,
                )
                k0 = pl.multiple_of((SLOT_ROW + chunk * 3) * LANES, LANES)
                acc_slot = acc_slot + gather_sum(placed, hot[:, pl.ds(k0, 3 * LANES)])
            return acc, acc_slot

        return lax.fori_loop(0, PAIR_CHUNKS // 8, chunk_group, (acc, jnp.zeros((8 * PEERS, LANES), F32)))

    def finish(turn, acc, vec):
        placed = []
        for k in range(PEERS + 1):
            if k < PEERS:
                got = recv_r[turn, k] * spread(list_live[k : k + 1, :])
            else:
                got = pltpu.roll(jnp.where(lane < 64, recv_r[turn, UP], recv_r[turn, DOWN]), 5, 0)
            top, rest = split(got)
            y8 = jnp.where(row < 3, top, pltpu.roll(rest, 3, 0))
            block = spread(ids[LIST_ROW + k : LIST_ROW + k + 1, :] >> 7)
            placed.append(place(y8, block, 8, 64))
        k0, k1 = LIST_ROW * LANES, (LIST_ROW + PEERS + 1) * LANES
        back = gather_sum(jnp.concatenate(placed, axis=1), hot[:, k0:k1])
        total[...] = acc[:64] + back
        return [
            mass[...] * vec[m] + (total[pl.ds(m, 8, stride=8), :] + total[pl.ds(m + 3, 8, stride=8), :])
            for m in range(3)
        ]

    def send_values(turn, vec):
        fill_own(vec)
        offer(turn)

    def rows_of(values):
        out = jnp.zeros((8, LANES), F32)
        for i, value in enumerate(values):
            out = jnp.where(row == i, jnp.sum(value, axis=0, keepdims=True), out)
        return out

    def dot(a, b):
        return a[0] * b[0] + a[1] * b[1] + a[2] * b[2]

    def start_sub(turn, mine):
        sum_send[turn, 0] = mine
        out = [
            pltpu.make_async_remote_copy(
                src_ref=sum_send.at[turn, 0], dst_ref=sum_a.at[turn, j - 1], send_sem=ss_sem.at[turn, j - 1],
                recv_sem=ra_sem.at[turn, j - 1], device_id=sub_peer(j), device_id_type=MESH,
            )
            for j in range(1, 8)
        ]
        for copy in out:
            copy.start()
        return out

    def start_region(turn, first):
        for copy in first:
            copy.wait_recv()
        sum_send[turn, 1] = sum_send[turn, 0] + sum(sum_a[turn, j] for j in range(7))
        out = [
            pltpu.make_async_remote_copy(
                src_ref=sum_send.at[turn, 1], dst_ref=sum_b.at[turn, j - 1], send_sem=ss_sem.at[turn, 6 + j],
                recv_sem=rb_sem.at[turn, j - 1], device_id=region_peer(j), device_id_type=MESH,
            )
            for j in range(1, 16)
        ]
        for copy in out:
            copy.start()
        return out

    def end_sums(turn, second):
        for copy in second:
            copy.wait_recv()
        whole = sum_send[turn, 1] + sum(sum_b[turn, j] for j in range(15))
        whole = jnp.sum(whole, axis=1, keepdims=True)
        return [whole[i : i + 1, :] for i in range(3)]

    def operate(turn, vec, early, late):
        copies = exchange(send_v, recv_v, sv_sem, rv_sem, turn, 1)
        for copy in copies:
            copy.start()
        started.extend(copies)
        early()
        recv_v[turn, 0] = send_v[turn, 0]
        for copy in copies:
            copy.wait_recv()
        halo_lookups(turn)
        acc, acc_slot = contacts(turn, jnp.zeros((OWN_ROWS, LANES), F32))
        acc = elements(acc)
        rim = acc[64:72]
        rim = rim + pltpu.roll(rim, 5, 0)
        for k in range(PEERS):
            out = acc_slot[8 * k : 8 * k + 8]
            out = out + pltpu.roll(out, 5, 0)
            if k in (UP, DOWN):
                out = jnp.where(row < 3, out, pltpu.roll(rim, 3, 0))
            if k == 0:
                recv_r[turn, 0] = out
            else:
                send_r[turn, k] = out
        copies = exchange(send_r, recv_r, sr_sem, rr_sem, turn, -1)
        for copy in copies:
            copy.start()
        started.extend(copies)
        late()
        for copy in copies:
            copy.wait_recv()
        return finish(turn, acc, vec)

    rhs = [vert[m] for m in range(3)]
    d0 = precondition(rhs)
    send_values(0, d0)

    def prepare():
        for copy in copies[6:10]:
            copy.wait()
        for chunk in range(ELEM_CHUNKS):
            ids[4 * chunk : 4 * chunk + 4, :] = enodes[:, chunk * LANES : (chunk + 1) * LANES]
        ids[POINT_ROW : POINT_ROW + PAIR_CHUNKS, :] = point[...]
        for chunk in range(PAIR_CHUNKS):
            ids[SLOT_ROW + 3 * chunk : SLOT_ROW + 3 * chunk + 3, :] = slot[:, chunk * LANES : (chunk + 1) * LANES]

        tall = lax.broadcasted_iota(jnp.int32, (LANES, LANES), 0)

        def hot_group(g, carry):
            low8 = ids[pl.ds(pl.multiple_of(g * 8, 8), 8), :] & 127
            for q in range(8):
                hit = jnp.broadcast_to(low8[q : q + 1, :], (LANES, LANES)) == tall
                k0 = pl.multiple_of((g * 8 + q) * LANES, LANES)
                hot[:, pl.ds(k0, LANES)] = jnp.where(hit, 1.0, 0.0).astype(BF16)
            return carry

        lax.fori_loop(0, ID_ROWS // 8, hot_group, 0)
        own_lookups()
        for copy in copies[10:]:
            copy.wait()

    pl.semaphore_wait(barrier, len(greeted))
    u0 = operate(0, d0, prepare, lambda: None)

    first_sub = start_sub(0, rows_of([dot(rhs, d0), dot(d0, u0)]))
    w = precondition(u0)
    send_values(1, w)
    held = {}

    def between():
        own_lookups()
        held["region"] = start_region(0, first_sub)

    v = operate(1, w, between, lambda: None)
    gamma0, curve0, _ = end_sums(0, held["region"])
    alpha = gamma0 / curve0
    r1 = [rhs[m] - alpha * u0[m] for m in range(3)]
    s1 = [d0[m] - alpha * w[m] for m in range(3)]
    a1 = [u0[m] - alpha * v[m] for m in range(3)]
    second_sub = start_sub(1, rows_of([dot(r1, s1), dot(s1, a1), dot(s1, u0)]))
    second_region = start_region(1, second_sub)
    gamma1, same, cross = end_sums(1, second_region)
    beta = gamma1 / gamma0
    curve1 = same + 2.0 * beta * cross + beta * beta * curve0
    alpha1 = gamma1 / curve1
    for m in range(3):
        d1 = s1[m] + beta * d0[m]
        image = a1[m] + beta * u0[m]
        out_s = alpha * d0[m] + alpha1 * d1
        out_r = r1[m] - alpha1 * image
        for j in range(8):
            sol_ref[m : m + 1, j * LANES : (j + 1) * LANES] = out_s[j : j + 1, :]
            res_ref[m : m + 1, j * LANES : (j + 1) * LANES] = out_r[j : j + 1, :]
    for copy in started + first_sub + held["region"] + second_sub + second_region:
        copy.wait_send()


def per_device(
    right_side, node_mass, precond, elem_hess, elem_nodes, halo_lists, contact_hess, pair_point, pair_slot,
    pair_live, contact_send, send_counts,
):
    any_space = pl.BlockSpec(memory_space=pl.ANY)
    vmem = pl.BlockSpec(memory_space=pltpu.VMEM)
    args = (
        right_side, node_mass.reshape(8, LANES), precond, elem_hess, elem_nodes, halo_lists, contact_hess,
        pair_point.reshape(-1, LANES), pair_slot, pair_live.reshape(-1, LANES), contact_send[0], send_counts,
    )
    out = jax.ShapeDtypeStruct(right_side.shape, F32)
    dma = pltpu.SemaphoreType.DMA
    return pl.pallas_call(
        kernel,
        out_shape=(out, out),
        in_specs=[any_space] * len(args),
        out_specs=(vmem, vmem),
        scratch_shapes=[pltpu.VMEM(a.shape, a.dtype) for a in args]
        + [
            pltpu.VMEM((ID_ROWS, LANES), jnp.int32),
            pltpu.VMEM((LANES, ID_ROWS * LANES), BF16),
            pltpu.VMEM((3, 8, LANES), F32),
            pltpu.VMEM((3, NODE_BLOCKS, 8, LANES), F32),
            pltpu.VMEM((3, PEERS, 8, LANES), F32),
            pltpu.VMEM((3, 4 * ELEM_CHUNKS, LANES), F32),
            pltpu.VMEM((3, PAIR_CHUNKS, LANES), F32),
            pltpu.VMEM((12, 8, LANES), F32),
            pltpu.VMEM((64, LANES), F32),
            pltpu.VMEM((2, PEERS, 8, LANES), F32),
            pltpu.VMEM((2, PEERS, 8, LANES), F32),
            pltpu.VMEM((2, PEERS, 8, LANES), F32),
            pltpu.VMEM((2, PEERS, 8, LANES), F32),
            pltpu.VMEM((2, 2, 8, LANES), F32),
            pltpu.VMEM((2, 7, 8, LANES), F32),
            pltpu.VMEM((2, 15, 8, LANES), F32),
            dma((len(args),)),
            dma((2, PEERS)),
            dma((2, PEERS)),
            dma((2, PEERS)),
            dma((2, PEERS)),
            dma((2, 22)),
            dma((2, 7)),
            dma((2, 15)),
        ],
        compiler_params=pltpu.CompilerParams(
            collective_id=0, has_side_effects=True, vmem_limit_bytes=40 * 1024 * 1024
        ),
    )(*args)


def solution(mesh):
    both = P(None, AXES)
    return jax.shard_map(
        per_device,
        mesh=mesh,
        in_specs=(
            both, P(AXES), both, both, both, both, both, P(AXES), both, P(AXES), P(AXES, None, None), P(AXES, None),
        ),
        out_specs=(both, both),
        check_vma=False,
    )
```

```python
import jax
import jax.numpy as jnp
from jax import lax
from jax.experimental import pallas as pl
from jax.experimental.pallas import tpu as pltpu
from jax.sharding import PartitionSpec as P

MESH = pl.DeviceIdType.MESH
AXES = ("region", "sub")
F32 = jnp.float32
BF16 = jnp.bfloat16
LANES = 128
OFFSETS = (0, 1, 2, 3, 4, -1, -2, -3, -4, 64, 65, 63)
PEERS = len(OFFSETS)
UP, DOWN = 1, 5
NODE_BLOCKS = 8
ELEM_CHUNKS = 32
PAIR_CHUNKS = 16
ELEM_ROW, POINT_ROW, SLOT_ROW, LIST_ROW, ID_ROWS = 0, 128, 144, 192, 208
HALO_ROW = PEERS
OWN_ROWS = 80


def spread(row):
    return jnp.broadcast_to(row, (8, LANES))


def pick(tables, ids):
    block, lane = ids >> 7, ids & 127
    found = [jnp.zeros(ids.shape, F32) for _ in range(3)]
    for h in range(len(tables[0])):
        hit = block == h
        for m in range(3):
            value = jnp.take_along_axis(tables[m][h], lane, axis=1, mode="promise_in_bounds")
            found[m] = jnp.where(hit, value, found[m])
    return found


def block_product(hess, start, z, row):
    lanes = pl.ds(start, LANES)
    low = row < 4
    acc0 = acc1 = acc2 = None
    for j in range(6):
        za, zb = z[2 * j], z[2 * j + 1]
        t0 = hess[24 * j : 24 * j + 8, lanes] * za
        t1 = hess[24 * j + 8 : 24 * j + 16, lanes] * jnp.where(low, za, zb)
        t2 = hess[24 * j + 16 : 24 * j + 24, lanes] * zb
        if j == 0:
            acc0, acc1, acc2 = t0, t1, t2
        else:
            acc0, acc1, acc2 = acc0 + t0, acc1 + t1, acc2 + t2
    first = acc0 + pltpu.roll(jnp.where(low, acc2, acc1), 4, 0)
    last = acc1 + pltpu.roll(acc2, 4, 0)
    return first, last


def split(x):
    top = x.astype(BF16).astype(F32)
    return top, x - top


def vertex_rows(first, last, row):
    f0, f1 = split(first)
    l0, l1 = split(last)
    near = row < 3
    a0 = jnp.where(near, f0, pltpu.roll(f1, 3, 0))
    a1 = jnp.where(near, pltpu.roll(f0, 5, 0), f1)
    fl0 = jnp.where(row < 1, l0, f0)
    fl1 = jnp.where(row < 1, l1, f1)
    a2 = jnp.where(near, pltpu.roll(fl0, 2, 0), pltpu.roll(fl1, 5, 0))
    a3 = jnp.where(near, pltpu.roll(l0, 7, 0), pltpu.roll(l1, 2, 0))
    return a0, a1, a2, a3


def place(y8, block, count, rows):
    parts = [jnp.where(block == h, y8, 0.0) for h in range(count)]
    if rows > 8 * count:
        parts.append(jnp.zeros((rows - 8 * count, LANES), F32))
    return jnp.concatenate(parts, axis=0).astype(BF16)


def gather_sum(placed, hot):
    return lax.dot_general(placed, hot, (((1,), (1,)), ((), ())), preferred_element_type=F32)


def kernel(
    right_hbm, mass_hbm, precond_hbm, ehess_hbm, enodes_hbm, halo_hbm, chess_hbm, point_hbm, slot_hbm,
    live_hbm, list_hbm, count_hbm,
    out_ref,
    right, mass, precond, ehess, enodes, halo, chess, point, slot, live, lists, count,
    ids, hot, ztab, own_tab, got_tab, zelem, zpoint, vert, total,
    yelem, ypoint, yslot, send_v, recv_v, send_r, recv_r, send_h, recv_h, sum_send, sum_a, sum_b,
    in_sem, sv_sem, rv_sem, sr_sem, rr_sem, sh_sem, rh_sem, ss_sem, ra_sem, rb_sem,
):
    region, sub = lax.axis_index("region"), lax.axis_index("sub")
    part = region * 8 + sub

    def device(offset):
        q = lax.rem(part + offset + 128, 128)
        return (lax.div(q, 8), lax.rem(q, 8))

    def sub_peer(j):
        return (region, lax.rem(sub + j, 8))

    def region_peer(j):
        return (lax.rem(region + j, 16), sub)

    barrier = pltpu.get_barrier_semaphore()
    greeted = [device(o) for o in OFFSETS[1:]] + [sub_peer(j) for j in range(1, 8)]
    greeted += [region_peer(j) for j in range(1, 16) if j != 8]
    for peer in greeted:
        pl.semaphore_signal(barrier, inc=1, device_id=peer, device_id_type=MESH)

    pairs = [
        (right_hbm, right), (precond_hbm, precond), (list_hbm, lists), (count_hbm, count), (halo_hbm, halo),
        (mass_hbm, mass), (enodes_hbm, enodes), (point_hbm, point), (slot_hbm, slot), (live_hbm, live),
        (chess_hbm, chess), (ehess_hbm, ehess),
    ]
    copies = [pltpu.make_async_copy(src, dst, in_sem.at[i]) for i, (src, dst) in enumerate(pairs)]
    for copy in copies:
        copy.start()

    row = lax.broadcasted_iota(jnp.int32, (8, LANES), 0)
    lane = lax.broadcasted_iota(jnp.int32, (8, LANES), 1)

    for copy in copies[:6]:
        copy.wait()
    for m in range(3):
        for j in range(8):
            vert[m, j : j + 1, :] = right[m : m + 1, j * LANES : (j + 1) * LANES]
    for k in range(9):
        for j in range(8):
            vert[3 + k, j : j + 1, :] = precond[k : k + 1, j * LANES : (j + 1) * LANES]

    def precondition(vec):
        return [sum(vert[3 + 3 * m + l] * vec[l] for l in range(3)) for m in range(3)]

    ids[LIST_ROW : LIST_ROW + PEERS, :] = lists[:, 0, :]
    ids[LIST_ROW + PEERS : LIST_ROW + PEERS + 1, :] = jnp.concatenate([halo[1:2, :], halo[0:1, :]], axis=1)
    ids[LIST_ROW + PEERS + 1 : ID_ROWS, :] = jnp.zeros((ID_ROWS - LIST_ROW - PEERS - 1, LANES), jnp.int32)
    diag = lax.broadcasted_iota(jnp.int32, (16, PEERS), 0) == lax.broadcasted_iota(jnp.int32, (16, PEERS), 1)
    limit = jnp.sum(jnp.where(diag, jnp.broadcast_to(count[...], (16, PEERS)), 0).astype(F32), axis=1, keepdims=True)
    wide_row = lax.broadcasted_iota(jnp.int32, (16, LANES), 0)
    wide_lane = lax.broadcasted_iota(jnp.int32, (16, LANES), 1).astype(F32)
    list_live = jnp.where((wide_lane < limit) | (wide_row == HALO_ROW), 1.0, 0.0)

    def fill_own(vec):
        for m in range(3):
            for h in range(NODE_BLOCKS):
                own_tab[m, h] = spread(vec[m][h : h + 1, :])

    own_tables = [[own_tab.at[m, h] for h in range(NODE_BLOCKS)] for m in range(3)]
    got_tables = [[got_tab.at[m, k] for k in range(PEERS)] for m in range(3)]

    def read(tables):
        return [[t[...] for t in line] for line in tables]

    def offer(turn):
        got = [[], [], []]
        for g in range(2):
            found = pick(read(own_tables), ids[LIST_ROW + 8 * g : LIST_ROW + 8 * g + 8, :])
            for m in range(3):
                got[m].append(found[m] * list_live[8 * g : 8 * g + 8, :])
        for k in range(PEERS):
            for m in range(3):
                send_v[turn, k, m : m + 1, :] = got[m][k // 8][k % 8 : k % 8 + 1, :]
        for k in (UP, DOWN):
            for m in range(3):
                h = HALO_ROW
                send_v[turn, k, 3 + m : 4 + m, :] = got[m][h // 8][h % 8 : h % 8 + 1, :]

    def exchange(src, dst, s_sem, r_sem, turn, sign):
        return [
            pltpu.make_async_remote_copy(
                src_ref=src.at[turn, k], dst_ref=dst.at[turn, k], send_sem=s_sem.at[turn, k],
                recv_sem=r_sem.at[turn, k], device_id=device(sign * OFFSETS[k]), device_id_type=MESH,
            )
            for k in range(1, PEERS)
        ]

    started = []

    def own_lookups():
        def elem_group(g, carry):
            rows = pl.ds(pl.multiple_of(g * 8, 8), 8)
            found = pick(read(own_tables), ids[rows, :])
            for m in range(3):
                zelem[m, rows, :] = found[m]
            return carry

        lax.fori_loop(0, 16, elem_group, 0)
        for g in range(2):
            found = pick(read(own_tables), ids[POINT_ROW + 8 * g : POINT_ROW + 8 * g + 8, :])
            for m in range(3):
                zpoint[m, 8 * g : 8 * g + 8, :] = found[m]

    def halo_lookups(turn):
        for m in range(3):
            ztab[m] = jnp.where(lane < 64, spread(recv_v[turn, UP, 3 + m : 4 + m, :]), spread(recv_v[turn, DOWN, 3 + m : 4 + m, :]))

        def elem_group(g, carry):
            rows = pl.ds(pl.multiple_of(g * 8, 8), 8)
            here = ids[rows, :]
            hit = (here >> 7) == NODE_BLOCKS
            for m in range(3):
                value = jnp.take_along_axis(ztab[m], here & 127, axis=1, mode="promise_in_bounds")
                zelem[m, rows, :] = jnp.where(hit, value, zelem[m, rows, :])
            return carry

        lax.fori_loop(0, 16, elem_group, 0)

    def energy(first, last, z):
        low = z[0]
        for c in range(1, 8):
            low = jnp.where(row == c, z[c], low)
        high = jnp.zeros((8, LANES), F32)
        for c in range(4):
            high = jnp.where(row == c, z[8 + c], high)
        return first * low + last * high

    def element_products():
        def chunk_group(c, power):
            for q2 in range(4):
                rows = pl.ds(pl.multiple_of(c * 32 + q2 * 8, 8), 8)
                z8 = [zelem[m, rows, :] for m in range(3)]
                for half in range(2):
                    chunk = c * 8 + q2 * 2 + half
                    start = pl.multiple_of(chunk * LANES, LANES)
                    z = [spread(z8[m][half * 4 + a : half * 4 + a + 1, :]) for a in range(4) for m in range(3)]
                    first, last = block_product(ehess, start, z, row)
                    power = power + energy(first, last, z)
                    for a, y8 in enumerate(vertex_rows(first, last, row)):
                        yelem[chunk * 4 + a] = y8
            return power

        return lax.fori_loop(0, ELEM_CHUNKS // 8, chunk_group, jnp.zeros((8, LANES), F32))

    def contact_products(turn):
        for k in range(PEERS):
            for m in range(3):
                got_tab[m, k] = spread(recv_v[turn, k, m : m + 1, :])

        def chunk_group(c, power):
            rows = pl.ds(pl.multiple_of(c * 8, 8), 8)
            zp = [zpoint[m, rows, :] for m in range(3)]
            alive = live[rows, :].astype(F32)
            zs = [
                pick(read(got_tables), ids[pl.ds(pl.multiple_of(SLOT_ROW + c * 24 + 8 * i, 8), 8), :]) for i in range(3)
            ]
            for q in range(8):
                chunk = c * 8 + q
                start = pl.multiple_of(chunk * LANES, LANES)
                z = [spread(zp[m][q : q + 1, :]) for m in range(3)]
                where = [(3 * q + a) for a in range(3)]
                z += [spread(zs[w // 8][m][w % 8 : w % 8 + 1, :]) for w in where for m in range(3)]
                first, last = block_product(chess, start, z, row)
                gate = spread(alive[q : q + 1, :])
                first, last = first * gate, last * gate
                power = power + energy(first, last, z)
                ys = vertex_rows(first, last, row)
                ypoint[chunk] = ys[0]
                for a in range(3):
                    yslot[chunk * 3 + a] = ys[1 + a]
            return power

        return lax.fori_loop(0, PAIR_CHUNKS // 8, chunk_group, jnp.zeros((8, LANES), F32))

    def scatter(held, base, units, blocks, rows, acc):
        def step(g, acc):
            block8 = ids[pl.ds(pl.multiple_of(base + g * 8, 8), 8), :] >> 7
            placed = [place(held[g * 8 + u], spread(block8[u : u + 1, :]), blocks, rows) for u in range(8)]
            k0 = pl.multiple_of((base + g * 8) * LANES, 8 * LANES)
            return acc + gather_sum(jnp.concatenate(placed, axis=1), hot[:, pl.ds(k0, 8 * LANES)])

        return lax.fori_loop(0, units // 8, step, acc)

    def finish(turn, acc, vec):
        placed = []
        for k in range(PEERS + 1):
            if k < PEERS:
                got = recv_r[turn, k] * spread(list_live[k : k + 1, :])
            else:
                got = jnp.where(lane < 64, recv_h[turn, 0], recv_h[turn, 1])
            top, rest = split(got)
            y8 = jnp.where(row < 3, top, pltpu.roll(rest, 3, 0))
            block = spread(ids[LIST_ROW + k : LIST_ROW + k + 1, :] >> 7)
            placed.append(place(y8, block, 8, 64))
        k0, k1 = LIST_ROW * LANES, (LIST_ROW + PEERS + 1) * LANES
        back = gather_sum(jnp.concatenate(placed, axis=1), hot[:, k0:k1])
        total[...] = acc[:64] + back
        return [
            mass[...] * vec[m] + (total[pl.ds(m, 8, stride=8), :] + total[pl.ds(m + 3, 8, stride=8), :])
            for m in range(3)
        ]

    def send_values(turn, vec):
        fill_own(vec)
        offer(turn)

    def rows_of(values):
        out = jnp.zeros((8, LANES), F32)
        for i, value in enumerate(values):
            out = jnp.where(row == i, jnp.sum(value, axis=0, keepdims=True), out)
        return out

    def dot(a, b):
        return a[0] * b[0] + a[1] * b[1] + a[2] * b[2]

    def start_sub(turn, mine):
        sum_send[turn, 0] = mine
        out = [
            pltpu.make_async_remote_copy(
                src_ref=sum_send.at[turn, 0], dst_ref=sum_a.at[turn, j - 1], send_sem=ss_sem.at[turn, j - 1],
                recv_sem=ra_sem.at[turn, j - 1], device_id=sub_peer(j), device_id_type=MESH,
            )
            for j in range(1, 8)
        ]
        for copy in out:
            copy.start()
        return out

    def start_region(turn, first):
        for copy in first:
            copy.wait_recv()
        sum_send[turn, 1] = sum_send[turn, 0] + sum(sum_a[turn, j] for j in range(7))
        out = [
            pltpu.make_async_remote_copy(
                src_ref=sum_send.at[turn, 1], dst_ref=sum_b.at[turn, j - 1], send_sem=ss_sem.at[turn, 6 + j],
                recv_sem=rb_sem.at[turn, j - 1], device_id=region_peer(j), device_id_type=MESH,
            )
            for j in range(1, 16)
        ]
        for copy in out:
            copy.start()
        return out

    def end_sums(turn, second):
        for copy in second:
            copy.wait_recv()
        whole = sum_send[turn, 1] + sum(sum_b[turn, j] for j in range(15))
        whole = jnp.sum(whole, axis=1, keepdims=True)
        return [whole[i : i + 1, :] for i in range(3)]

    def operate(turn, vec, early, sums):
        copies = exchange(send_v, recv_v, sv_sem, rv_sem, turn, 1)
        for copy in copies:
            copy.start()
        started.extend(copies)
        early()
        own_lookups()
        recv_v[turn, 0] = send_v[turn, 0]
        for k in (UP, DOWN):
            copies[k - 1].wait_recv()
        halo_lookups(turn)
        power = element_products()
        for k in range(1, PEERS):
            if k not in (UP, DOWN):
                copies[k - 1].wait_recv()
        power = power + contact_products(turn)
        power = power + mass[...] * dot(vec, vec)
        sub_copies = start_sub(turn, rows_of([power] + sums))

        acc_slot = scatter(yslot, SLOT_ROW, 3 * PAIR_CHUNKS, PEERS, 8 * PEERS, jnp.zeros((8 * PEERS, LANES), F32))
        for k in range(PEERS):
            out = acc_slot[8 * k : 8 * k + 8]
            out = out + pltpu.roll(out, 5, 0)
            if k == 0:
                recv_r[turn, 0] = out
            else:
                send_r[turn, k] = out
        back = exchange(send_r, recv_r, sr_sem, rr_sem, turn, -1)
        for copy in back:
            copy.start()
        acc = scatter(yelem, ELEM_ROW, 4 * ELEM_CHUNKS, 9, OWN_ROWS, jnp.zeros((OWN_ROWS, LANES), F32))
        rim = acc[64:72]
        send_h[turn] = rim + pltpu.roll(rim, 5, 0)
        rims = [
            pltpu.make_async_remote_copy(
                src_ref=send_h.at[turn], dst_ref=recv_h.at[turn, i], send_sem=sh_sem.at[turn, i],
                recv_sem=rh_sem.at[turn, i], device_id=device(-OFFSETS[k]), device_id_type=MESH,
            )
            for i, k in enumerate((UP, DOWN))
        ]
        for copy in rims:
            copy.start()
        acc = scatter(ypoint, POINT_ROW, PAIR_CHUNKS, NODE_BLOCKS, OWN_ROWS, acc)
        region_copies = start_region(turn, sub_copies)
        for copy in rims + back:
            copy.wait_recv()
        image = finish(turn, acc, vec)
        started.extend(rims + back + sub_copies + region_copies)
        return image, end_sums(turn, region_copies)

    rhs = [vert[m] for m in range(3)]
    d0 = precondition(rhs)
    send_values(0, d0)

    def prepare():
        for copy in copies[6:10]:
            copy.wait()
        for chunk in range(ELEM_CHUNKS):
            ids[4 * chunk : 4 * chunk + 4, :] = enodes[:, chunk * LANES : (chunk + 1) * LANES]
        ids[POINT_ROW : POINT_ROW + PAIR_CHUNKS, :] = point[...]
        for chunk in range(PAIR_CHUNKS):
            ids[SLOT_ROW + 3 * chunk : SLOT_ROW + 3 * chunk + 3, :] = slot[:, chunk * LANES : (chunk + 1) * LANES]

        tall = lax.broadcasted_iota(jnp.int32, (LANES, LANES), 0)

        def hot_group(g, carry):
            low8 = ids[pl.ds(pl.multiple_of(g * 8, 8), 8), :] & 127
            for q in range(8):
                hit = jnp.broadcast_to(low8[q : q + 1, :], (LANES, LANES)) == tall
                k0 = pl.multiple_of((g * 8 + q) * LANES, LANES)
                hot[:, pl.ds(k0, LANES)] = jnp.where(hit, 1.0, 0.0).astype(BF16)
            return carry

        lax.fori_loop(0, ID_ROWS // 8, hot_group, 0)
        for copy in copies[10:]:
            copy.wait()

    pl.semaphore_wait(barrier, len(greeted))
    u0, (curve0, gamma0, _) = operate(0, d0, prepare, [dot(rhs, d0)])
    alpha = gamma0 / curve0
    r1 = [rhs[m] - alpha * u0[m] for m in range(3)]
    s1 = precondition(r1)
    send_values(1, s1)
    a1, (same, gamma1, cross) = operate(1, s1, lambda: None, [dot(r1, s1), dot(s1, u0)])
    beta = gamma1 / gamma0
    curve1 = same + 2.0 * beta * cross + beta * beta * curve0
    alpha1 = gamma1 / curve1
    for m in range(3):
        d1 = s1[m] + beta * d0[m]
        image = a1[m] + beta * u0[m]
        out_s = alpha * d0[m] + alpha1 * d1
        out_r = r1[m] - alpha1 * image
        for j in range(8):
            out_ref[m : m + 1, j * LANES : (j + 1) * LANES] = out_s[j : j + 1, :]
            out_ref[3 + m : 4 + m, j * LANES : (j + 1) * LANES] = out_r[j : j + 1, :]
    for copy in started:
        copy.wait_send()


def per_device(
    right_side, node_mass, precond, elem_hess, elem_nodes, halo_lists, contact_hess, pair_point, pair_slot,
    pair_live, contact_send, send_counts,
):
    any_space = pl.BlockSpec(memory_space=pl.ANY)
    vmem = pl.BlockSpec(memory_space=pltpu.VMEM)
    args = (
        right_side, node_mass.reshape(8, LANES), precond, elem_hess, elem_nodes, halo_lists, contact_hess,
        pair_point.reshape(-1, LANES), pair_slot, pair_live.reshape(-1, LANES), contact_send.swapaxes(0, 1), send_counts,
    )
    out = jax.ShapeDtypeStruct((6, right_side.shape[1]), F32)
    dma = pltpu.SemaphoreType.DMA
    both = pl.pallas_call(
        kernel,
        out_shape=out,
        in_specs=[any_space] * len(args),
        out_specs=vmem,
        scratch_shapes=[pltpu.VMEM(a.shape, a.dtype) for a in args]
        + [
            pltpu.VMEM((ID_ROWS, LANES), jnp.int32),
            pltpu.VMEM((LANES, ID_ROWS * LANES), BF16),
            pltpu.VMEM((3, 8, LANES), F32),
            pltpu.VMEM((3, NODE_BLOCKS, 8, LANES), F32),
            pltpu.VMEM((3, PEERS, 8, LANES), F32),
            pltpu.VMEM((3, 4 * ELEM_CHUNKS, LANES), F32),
            pltpu.VMEM((3, PAIR_CHUNKS, LANES), F32),
            pltpu.VMEM((12, 8, LANES), F32),
            pltpu.VMEM((64, LANES), F32),
            pltpu.VMEM((4 * ELEM_CHUNKS, 8, LANES), F32),
            pltpu.VMEM((PAIR_CHUNKS, 8, LANES), F32),
            pltpu.VMEM((3 * PAIR_CHUNKS, 8, LANES), F32),
            pltpu.VMEM((2, PEERS, 8, LANES), F32),
            pltpu.VMEM((2, PEERS, 8, LANES), F32),
            pltpu.VMEM((2, PEERS, 8, LANES), F32),
            pltpu.VMEM((2, PEERS, 8, LANES), F32),
            pltpu.VMEM((2, 8, LANES), F32),
            pltpu.VMEM((2, 2, 8, LANES), F32),
            pltpu.VMEM((2, 2, 8, LANES), F32),
            pltpu.VMEM((2, 7, 8, LANES), F32),
            pltpu.VMEM((2, 15, 8, LANES), F32),
            dma((len(args),)),
            dma((2, PEERS)),
            dma((2, PEERS)),
            dma((2, PEERS)),
            dma((2, PEERS)),
            dma((2, 2)),
            dma((2, 2)),
            dma((2, 22)),
            dma((2, 7)),
            dma((2, 15)),
        ],
        compiler_params=pltpu.CompilerParams(
            collective_id=0, has_side_effects=True, vmem_limit_bytes=60 * 1024 * 1024
        ),
    )(*args)
    return both[:3], both[3:]


def solution(mesh):
    both = P(None, AXES)
    return jax.shard_map(
        per_device,
        mesh=mesh,
        in_specs=(
            both, P(AXES), both, both, both, both, both, P(AXES), both, P(AXES), P(AXES, None, None), P(AXES, None),
        ),
        out_specs=(both, both),
        check_vma=False,
    )
```

```python
import jax
import jax.numpy as jnp
from jax import lax
from jax.experimental import pallas as pl
from jax.experimental.pallas import tpu as pltpu
from jax.sharding import PartitionSpec as P

MESH = pl.DeviceIdType.MESH
AXES = ("region", "sub")
F32 = jnp.float32
BF16 = jnp.bfloat16
LANES = 128
OFFSETS = (0, 1, 2, 3, 4, -1, -2, -3, -4, 64, 65, 63)
PEERS = len(OFFSETS)
UP, DOWN = 1, 5
NODE_BLOCKS = 8
ELEM_CHUNKS = 32
PAIR_CHUNKS = 16
ELEM_ROW, POINT_ROW, SLOT_ROW, LIST_ROW, ID_ROWS = 0, 128, 144, 192, 208
HALO_ROW = PEERS
OWN_ROWS = 80


def spread(row):
    return jnp.broadcast_to(row, (8, LANES))


def pick(tables, ids):
    block, lane = ids >> 7, ids & 127
    found = [jnp.zeros(ids.shape, F32) for _ in range(3)]
    for h in range(len(tables[0])):
        hit = block == h
        for m in range(3):
            value = jnp.take_along_axis(tables[m][h], lane, axis=1, mode="promise_in_bounds")
            found[m] = jnp.where(hit, value, found[m])
    return found


def block_product(hess, start, z, row):
    lanes = pl.ds(start, LANES)
    low = row < 4
    acc0 = acc1 = acc2 = None
    for j in range(6):
        za, zb = z[2 * j], z[2 * j + 1]
        t0 = hess[24 * j : 24 * j + 8, lanes] * za
        t1 = hess[24 * j + 8 : 24 * j + 16, lanes] * jnp.where(low, za, zb)
        t2 = hess[24 * j + 16 : 24 * j + 24, lanes] * zb
        if j == 0:
            acc0, acc1, acc2 = t0, t1, t2
        else:
            acc0, acc1, acc2 = acc0 + t0, acc1 + t1, acc2 + t2
    first = acc0 + pltpu.roll(jnp.where(low, acc2, acc1), 4, 0)
    last = acc1 + pltpu.roll(acc2, 4, 0)
    return first, last


def split(x):
    top = x.astype(BF16).astype(F32)
    return top, x - top


def vertex_rows(first, last, row):
    f0, f1 = split(first)
    l0, l1 = split(last)
    near = row < 3
    a0 = jnp.where(near, f0, pltpu.roll(f1, 3, 0))
    a1 = jnp.where(near, pltpu.roll(f0, 5, 0), f1)
    fl0 = jnp.where(row < 1, l0, f0)
    fl1 = jnp.where(row < 1, l1, f1)
    a2 = jnp.where(near, pltpu.roll(fl0, 2, 0), pltpu.roll(fl1, 5, 0))
    a3 = jnp.where(near, pltpu.roll(l0, 7, 0), pltpu.roll(l1, 2, 0))
    return a0, a1, a2, a3


def place(y8, block, count, rows):
    parts = [jnp.where(block == h, y8, 0.0) for h in range(count)]
    if rows > 8 * count:
        parts.append(jnp.zeros((rows - 8 * count, LANES), F32))
    return jnp.concatenate(parts, axis=0).astype(BF16)


def gather_sum(placed, hot):
    return jnp.dot(placed, hot, preferred_element_type=F32)


def kernel(
    right_hbm, mass_hbm, precond_hbm, ehess_hbm, enodes_hbm, halo_hbm, chess_hbm, point_hbm, slot_hbm,
    live_hbm, list_hbm, count_hbm,
    out_ref,
    right, mass, precond, ehess, enodes, halo, chess, point, slot, live, lists, count,
    ids, hot, ztab, own_tab, got_tab, zelem, zpoint, vert, total,
    yelem, ypoint, yslot, send_v, recv_v, send_r, recv_r, send_h, recv_h, sum_send, sum_a, sum_b,
    in_sem, sv_sem, rv_sem, sr_sem, rr_sem, sh_sem, rh_sem, ss_sem, ra_sem, rb_sem,
):
    region, sub = lax.axis_index("region"), lax.axis_index("sub")
    part = region * 8 + sub

    known = {}

    def device(offset):
        offset %= 128
        if offset not in known:
            q = lax.rem(part + offset, 128)
            known[offset] = (lax.div(q, 8), lax.rem(q, 8))
        return known[offset]

    def sub_peer(j):
        return (region, lax.rem(sub + j, 8))

    def region_peer(j):
        return (lax.rem(region + j, 16), sub)

    barrier = pltpu.get_barrier_semaphore()
    greeted = [device(o) for o in OFFSETS[1:]] + [sub_peer(j) for j in range(1, 8)]
    greeted += [region_peer(j) for j in range(1, 16) if j != 8]
    for peer in greeted:
        pl.semaphore_signal(barrier, inc=1, device_id=peer, device_id_type=MESH)

    pairs = [
        (right_hbm, right), (precond_hbm, precond), (list_hbm, lists), (count_hbm, count), (halo_hbm, halo),
        (mass_hbm, mass), (enodes_hbm, enodes), (point_hbm, point), (slot_hbm, slot), (live_hbm, live),
        (chess_hbm, chess), (ehess_hbm, ehess),
    ]
    copies = [pltpu.make_async_copy(src, dst, in_sem.at[i]) for i, (src, dst) in enumerate(pairs)]
    for copy in copies:
        copy.start()

    row = lax.broadcasted_iota(jnp.int32, (8, LANES), 0)
    lane = lax.broadcasted_iota(jnp.int32, (8, LANES), 1)

    for copy in copies[:6]:
        copy.wait()
    for m in range(3):
        for j in range(8):
            vert[m, j : j + 1, :] = right[m : m + 1, j * LANES : (j + 1) * LANES]
    for k in range(9):
        for j in range(8):
            vert[3 + k, j : j + 1, :] = precond[k : k + 1, j * LANES : (j + 1) * LANES]

    def precondition(vec):
        return [sum(vert[3 + 3 * m + l] * vec[l] for l in range(3)) for m in range(3)]

    ids[LIST_ROW : LIST_ROW + PEERS, :] = lists[:, 0, :]
    ids[LIST_ROW + PEERS : LIST_ROW + PEERS + 1, :] = jnp.concatenate([halo[1:2, :], halo[0:1, :]], axis=1)
    ids[LIST_ROW + PEERS + 1 : ID_ROWS, :] = jnp.zeros((ID_ROWS - LIST_ROW - PEERS - 1, LANES), jnp.int32)
    diag = lax.broadcasted_iota(jnp.int32, (16, PEERS), 0) == lax.broadcasted_iota(jnp.int32, (16, PEERS), 1)
    limit = jnp.sum(jnp.where(diag, jnp.broadcast_to(count[...], (16, PEERS)), 0).astype(F32), axis=1, keepdims=True)
    wide_row = lax.broadcasted_iota(jnp.int32, (16, LANES), 0)
    wide_lane = lax.broadcasted_iota(jnp.int32, (16, LANES), 1).astype(F32)
    list_live = jnp.where((wide_lane < limit) | (wide_row == HALO_ROW), 1.0, 0.0)

    def fill_own(vec):
        for m in range(3):
            for h in range(NODE_BLOCKS):
                own_tab[m, h] = spread(vec[m][h : h + 1, :])

    own_tables = [[own_tab.at[m, h] for h in range(NODE_BLOCKS)] for m in range(3)]
    got_tables = [[got_tab.at[m, k] for k in range(PEERS)] for m in range(3)]

    def read(tables):
        return [[t[...] for t in line] for line in tables]

    def offer(turn):
        got = [[], [], []]
        for g in range(2):
            found = pick(read(own_tables), ids[LIST_ROW + 8 * g : LIST_ROW + 8 * g + 8, :])
            for m in range(3):
                got[m].append(found[m] * list_live[8 * g : 8 * g + 8, :])
        for k in range(PEERS):
            for m in range(3):
                send_v[turn, k, m : m + 1, :] = got[m][k // 8][k % 8 : k % 8 + 1, :]
        for k in (UP, DOWN):
            for m in range(3):
                h = HALO_ROW
                send_v[turn, k, 3 + m : 4 + m, :] = got[m][h // 8][h % 8 : h % 8 + 1, :]

    def exchange(src, dst, s_sem, r_sem, turn, sign):
        return [
            pltpu.make_async_remote_copy(
                src_ref=src.at[turn, k], dst_ref=dst.at[turn, k], send_sem=s_sem.at[turn, k],
                recv_sem=r_sem.at[turn, k], device_id=device(sign * OFFSETS[k]), device_id_type=MESH,
            )
            for k in range(1, PEERS)
        ]

    started = []

    def own_lookups():
        def elem_group(g, carry):
            rows = pl.ds(pl.multiple_of(g * 8, 8), 8)
            found = pick(read(own_tables), ids[rows, :])
            for m in range(3):
                zelem[m, rows, :] = found[m]
            return carry

        lax.fori_loop(0, 16, elem_group, 0)
        for g in range(2):
            found = pick(read(own_tables), ids[POINT_ROW + 8 * g : POINT_ROW + 8 * g + 8, :])
            for m in range(3):
                zpoint[m, 8 * g : 8 * g + 8, :] = found[m]

    def halo_lookups(turn):
        for m in range(3):
            ztab[m] = jnp.where(lane < 64, spread(recv_v[turn, UP, 3 + m : 4 + m, :]), spread(recv_v[turn, DOWN, 3 + m : 4 + m, :]))

        def elem_group(g, carry):
            rows = pl.ds(pl.multiple_of(g * 8, 8), 8)
            here = ids[rows, :]
            hit = (here >> 7) == NODE_BLOCKS
            for m in range(3):
                value = jnp.take_along_axis(ztab[m], here & 127, axis=1, mode="promise_in_bounds")
                zelem[m, rows, :] = jnp.where(hit, value, zelem[m, rows, :])
            return carry

        lax.fori_loop(0, 16, elem_group, 0)

    def energy(first, last, z):
        low = z[0]
        for c in range(1, 8):
            low = jnp.where(row == c, z[c], low)
        high = jnp.zeros((8, LANES), F32)
        for c in range(4):
            high = jnp.where(row == c, z[8 + c], high)
        return first * low + last * high

    def element_products():
        def chunk_group(c, power):
            for q2 in range(4):
                rows = pl.ds(pl.multiple_of(c * 32 + q2 * 8, 8), 8)
                z8 = [zelem[m, rows, :] for m in range(3)]
                for half in range(2):
                    chunk = c * 8 + q2 * 2 + half
                    start = pl.multiple_of(chunk * LANES, LANES)
                    z = [spread(z8[m][half * 4 + a : half * 4 + a + 1, :]) for a in range(4) for m in range(3)]
                    first, last = block_product(ehess, start, z, row)
                    power = power + energy(first, last, z)
                    for a, y8 in enumerate(vertex_rows(first, last, row)):
                        yelem[chunk * 4 + a] = y8
            return power

        return lax.fori_loop(0, ELEM_CHUNKS // 8, chunk_group, jnp.zeros((8, LANES), F32))

    def contact_products(turn):
        for k in range(PEERS):
            for m in range(3):
                got_tab[m, k] = spread(recv_v[turn, k, m : m + 1, :])

        power = jnp.zeros((8, LANES), F32)
        for c in range(PAIR_CHUNKS // 8):
            zp = [zpoint[m, 8 * c : 8 * c + 8, :] for m in range(3)]
            alive = live[8 * c : 8 * c + 8, :].astype(F32)
            first_slot = SLOT_ROW + 24 * c
            zs = [pick(read(got_tables), ids[first_slot + 8 * i : first_slot + 8 * i + 8, :]) for i in range(3)]
            for q in range(8):
                chunk = c * 8 + q
                z = [spread(zp[m][q : q + 1, :]) for m in range(3)]
                where = [(3 * q + a) for a in range(3)]
                z += [spread(zs[w // 8][m][w % 8 : w % 8 + 1, :]) for w in where for m in range(3)]
                first, last = block_product(chess, chunk * LANES, z, row)
                gate = spread(alive[q : q + 1, :])
                first, last = first * gate, last * gate
                power = power + energy(first, last, z)
                ys = vertex_rows(first, last, row)
                ypoint[chunk] = ys[0]
                for a in range(3):
                    yslot[chunk * 3 + a] = ys[1 + a]
        return power

    def scatter(held, base, blocks, rows):
        placed = []
        for u, y8 in enumerate(held):
            if u % 8 == 0:
                block8 = ids[base + u : base + u + 8, :] >> 7
            placed.append(place(y8, spread(block8[u % 8 : u % 8 + 1, :]), blocks, rows))
        k0, k1 = base * LANES, (base + len(held)) * LANES
        return gather_sum(jnp.concatenate(placed, axis=1), hot[k0:k1, :])

    def finish(turn, acc, vec):
        placed = []
        for k in range(PEERS + 1):
            if k < PEERS:
                got = recv_r[turn, k] * spread(list_live[k : k + 1, :])
            else:
                got = jnp.where(lane < 64, recv_h[turn, 0], recv_h[turn, 1])
            top, rest = split(got)
            y8 = jnp.where(row < 3, top, pltpu.roll(rest, 3, 0))
            placed.append(y8)
        back = scatter(placed, LIST_ROW, NODE_BLOCKS, 64)
        total[...] = acc[:64] + back
        return [
            mass[...] * vec[m] + (total[pl.ds(m, 8, stride=8), :] + total[pl.ds(m + 3, 8, stride=8), :])
            for m in range(3)
        ]

    def send_values(turn, vec):
        fill_own(vec)
        offer(turn)

    def rows_of(values):
        out = jnp.zeros((8, LANES), F32)
        for i, value in enumerate(values):
            out = jnp.where(row == i, jnp.sum(value, axis=0, keepdims=True), out)
        return out

    def dot(a, b):
        return a[0] * b[0] + a[1] * b[1] + a[2] * b[2]

    def start_sub(turn, mine):
        sum_send[turn, 0] = mine
        out = [
            pltpu.make_async_remote_copy(
                src_ref=sum_send.at[turn, 0], dst_ref=sum_a.at[turn, j - 1], send_sem=ss_sem.at[turn, j - 1],
                recv_sem=ra_sem.at[turn, j - 1], device_id=sub_peer(j), device_id_type=MESH,
            )
            for j in range(1, 8)
        ]
        for copy in out:
            copy.start()
        return out

    def start_region(turn, first):
        for copy in first:
            copy.wait_recv()
        sum_send[turn, 1] = sum_send[turn, 0] + sum(sum_a[turn, j] for j in range(7))
        out = [
            pltpu.make_async_remote_copy(
                src_ref=sum_send.at[turn, 1], dst_ref=sum_b.at[turn, j - 1], send_sem=ss_sem.at[turn, 6 + j],
                recv_sem=rb_sem.at[turn, j - 1], device_id=region_peer(j), device_id_type=MESH,
            )
            for j in range(1, 16)
        ]
        for copy in out:
            copy.start()
        return out

    def end_sums(turn, second):
        for copy in second:
            copy.wait_recv()
        whole = sum_send[turn, 1] + sum(sum_b[turn, j] for j in range(15))
        whole = jnp.sum(whole, axis=1, keepdims=True)
        return [whole[i : i + 1, :] for i in range(3)]

    def operate(turn, vec, early, late, sums):
        copies = exchange(send_v, recv_v, sv_sem, rv_sem, turn, 1)
        for copy in copies:
            copy.start()
        started.extend(copies)
        early()
        own_lookups()
        recv_v[turn, 0] = send_v[turn, 0]
        for k in (UP, DOWN):
            copies[k - 1].wait_recv()
        halo_lookups(turn)
        power = element_products()
        for k in range(1, PEERS):
            if k not in (UP, DOWN):
                copies[k - 1].wait_recv()
        power = power + contact_products(turn)
        power = power + mass[...] * dot(vec, vec)
        sub_copies = start_sub(turn, rows_of([power] + sums))

        acc_slot = scatter([yslot[u] for u in range(3 * PAIR_CHUNKS)], SLOT_ROW, PEERS, 8 * PEERS)
        for k in range(PEERS):
            out = acc_slot[8 * k : 8 * k + 8]
            out = out + pltpu.roll(out, 5, 0)
            if k == 0:
                recv_r[turn, 0] = out
            else:
                send_r[turn, k] = out
        back = exchange(send_r, recv_r, sr_sem, rr_sem, turn, -1)
        for copy in back:
            copy.start()
        own_rows = [yelem[u] for u in range(4 * ELEM_CHUNKS)] + [ypoint[u] for u in range(PAIR_CHUNKS)]
        acc = scatter(own_rows, ELEM_ROW, 9, OWN_ROWS)
        rim = acc[64:72]
        send_h[turn] = rim + pltpu.roll(rim, 5, 0)
        rims = [
            pltpu.make_async_remote_copy(
                src_ref=send_h.at[turn], dst_ref=recv_h.at[turn, i], send_sem=sh_sem.at[turn, i],
                recv_sem=rh_sem.at[turn, i], device_id=device(-OFFSETS[k]), device_id_type=MESH,
            )
            for i, k in enumerate((UP, DOWN))
        ]
        for copy in rims:
            copy.start()
        late()
        region_copies = start_region(turn, sub_copies)
        for copy in rims + back:
            copy.wait_recv()
        image = finish(turn, acc, vec)
        started.extend(rims + back + sub_copies + region_copies)
        return image, end_sums(turn, region_copies)

    rhs = [vert[m] for m in range(3)]
    d0 = precondition(rhs)
    send_values(0, d0)

    tall = lax.broadcasted_iota(jnp.int32, (LANES, LANES), 0)

    def hot_rows(first, last):
        def group(g, carry):
            low8 = ids[pl.ds(pl.multiple_of(g * 8, 8), 8), :] & 127
            for q in range(8):
                hit = jnp.broadcast_to(low8[q : q + 1, :], (LANES, LANES)) == tall
                k0 = pl.multiple_of((g * 8 + q) * LANES, LANES)
                hot[pl.ds(k0, LANES), :] = jnp.where(hit, 1.0, 0.0).astype(BF16).T
            return carry

        lax.fori_loop(first, last, group, 0)

    def prepare():
        for copy in copies[6:10]:
            copy.wait()
        for chunk in range(ELEM_CHUNKS):
            ids[4 * chunk : 4 * chunk + 4, :] = enodes[:, chunk * LANES : (chunk + 1) * LANES]
        ids[POINT_ROW : POINT_ROW + PAIR_CHUNKS, :] = point[...]
        for chunk in range(PAIR_CHUNKS):
            ids[SLOT_ROW + 3 * chunk : SLOT_ROW + 3 * chunk + 3, :] = slot[:, chunk * LANES : (chunk + 1) * LANES]

        hot_rows(0, LIST_ROW // 8)
        for copy in copies[10:]:
            copy.wait()

    pl.semaphore_wait(barrier, len(greeted))
    u0, (curve0, gamma0, _) = operate(0, d0, prepare, lambda: hot_rows(LIST_ROW // 8, ID_ROWS // 8), [dot(rhs, d0)])
    alpha = gamma0 / curve0
    r1 = [rhs[m] - alpha * u0[m] for m in range(3)]
    s1 = precondition(r1)
    send_values(1, s1)
    a1, (same, gamma1, cross) = operate(1, s1, lambda: None, lambda: None, [dot(r1, s1), dot(s1, u0)])
    beta = gamma1 / gamma0
    curve1 = same + 2.0 * beta * cross + beta * beta * curve0
    alpha1 = gamma1 / curve1
    for m in range(3):
        d1 = s1[m] + beta * d0[m]
        image = a1[m] + beta * u0[m]
        out_s = alpha * d0[m] + alpha1 * d1
        out_r = r1[m] - alpha1 * image
        for j in range(8):
            out_ref[m : m + 1, j * LANES : (j + 1) * LANES] = out_s[j : j + 1, :]
            out_ref[3 + m : 4 + m, j * LANES : (j + 1) * LANES] = out_r[j : j + 1, :]
    for copy in started:
        copy.wait_send()


def per_device(
    right_side, node_mass, precond, elem_hess, elem_nodes, halo_lists, contact_hess, pair_point, pair_slot,
    pair_live, contact_send, send_counts,
):
    any_space = pl.BlockSpec(memory_space=pl.ANY)
    vmem = pl.BlockSpec(memory_space=pltpu.VMEM)
    args = (
        right_side, node_mass.reshape(8, LANES), precond, elem_hess, elem_nodes, halo_lists, contact_hess,
        pair_point.reshape(-1, LANES), pair_slot, pair_live.reshape(-1, LANES), contact_send.swapaxes(0, 1), send_counts,
    )
    out = jax.ShapeDtypeStruct((6, right_side.shape[1]), F32)
    dma = pltpu.SemaphoreType.DMA
    both = pl.pallas_call(
        kernel,
        out_shape=out,
        in_specs=[any_space] * len(args),
        out_specs=vmem,
        scratch_shapes=[pltpu.VMEM(a.shape, a.dtype) for a in args]
        + [
            pltpu.VMEM((ID_ROWS, LANES), jnp.int32),
            pltpu.VMEM((ID_ROWS * LANES, LANES), BF16),
            pltpu.VMEM((3, 8, LANES), F32),
            pltpu.VMEM((3, NODE_BLOCKS, 8, LANES), F32),
            pltpu.VMEM((3, PEERS, 8, LANES), F32),
            pltpu.VMEM((3, 4 * ELEM_CHUNKS, LANES), F32),
            pltpu.VMEM((3, PAIR_CHUNKS, LANES), F32),
            pltpu.VMEM((12, 8, LANES), F32),
            pltpu.VMEM((64, LANES), F32),
            pltpu.VMEM((4 * ELEM_CHUNKS, 8, LANES), F32),
            pltpu.VMEM((PAIR_CHUNKS, 8, LANES), F32),
            pltpu.VMEM((3 * PAIR_CHUNKS, 8, LANES), F32),
            pltpu.VMEM((2, PEERS, 8, LANES), F32),
            pltpu.VMEM((2, PEERS, 8, LANES), F32),
            pltpu.VMEM((2, PEERS, 8, LANES), F32),
            pltpu.VMEM((2, PEERS, 8, LANES), F32),
            pltpu.VMEM((2, 8, LANES), F32),
            pltpu.VMEM((2, 2, 8, LANES), F32),
            pltpu.VMEM((2, 2, 8, LANES), F32),
            pltpu.VMEM((2, 7, 8, LANES), F32),
            pltpu.VMEM((2, 15, 8, LANES), F32),
            dma((len(args),)),
            dma((2, PEERS)),
            dma((2, PEERS)),
            dma((2, PEERS)),
            dma((2, PEERS)),
            dma((2, 2)),
            dma((2, 2)),
            dma((2, 22)),
            dma((2, 7)),
            dma((2, 15)),
        ],
        compiler_params=pltpu.CompilerParams(
            collective_id=0, has_side_effects=True, vmem_limit_bytes=60 * 1024 * 1024
        ),
    )(*args)
    return both[:3], both[3:]


def solution(mesh):
    both = P(None, AXES)
    return jax.shard_map(
        per_device,
        mesh=mesh,
        in_specs=(
            both, P(AXES), both, both, both, both, both, P(AXES), both, P(AXES), P(AXES, None, None), P(AXES, None),
        ),
        out_specs=(both, both),
        check_vma=False,
    )
```

```python
import jax
import jax.numpy as jnp
from jax import lax
from jax.experimental import pallas as pl
from jax.experimental.pallas import tpu as pltpu
from jax.sharding import PartitionSpec as P

MESH = pl.DeviceIdType.MESH
AXES = ("region", "sub")
F32 = jnp.float32
BF16 = jnp.bfloat16
LANES = 128
OFFSETS = (0, 1, 2, 3, 4, -1, -2, -3, -4, 64, 65, 63)
PEERS = len(OFFSETS)
UP, DOWN = 1, 5
NODE_BLOCKS = 8
ELEM_CHUNKS = 32
PAIR_CHUNKS = 16
ELEM_ROW, POINT_ROW, SLOT_ROW, LIST_ROW, ID_ROWS = 0, 128, 144, 192, 208
HALO_ROW = PEERS
OWN_ROWS = 80


def spread(row):
    return jnp.broadcast_to(row, (8, LANES))


def pick(tables, ids):
    block, lane = ids >> 7, ids & 127
    found = [jnp.zeros(ids.shape, F32) for _ in range(3)]
    for h in range(len(tables[0])):
        hit = block == h
        for m in range(3):
            value = jnp.take_along_axis(tables[m][h], lane, axis=1, mode="promise_in_bounds")
            found[m] = jnp.where(hit, value, found[m])
    return found


def block_product(hess, start, z, row):
    lanes = pl.ds(start, LANES)
    low = row < 4
    acc0 = acc1 = acc2 = None
    for j in range(6):
        za, zb = z[2 * j], z[2 * j + 1]
        t0 = hess[24 * j : 24 * j + 8, lanes] * za
        t1 = hess[24 * j + 8 : 24 * j + 16, lanes] * jnp.where(low, za, zb)
        t2 = hess[24 * j + 16 : 24 * j + 24, lanes] * zb
        if j == 0:
            acc0, acc1, acc2 = t0, t1, t2
        else:
            acc0, acc1, acc2 = acc0 + t0, acc1 + t1, acc2 + t2
    first = acc0 + pltpu.roll(jnp.where(low, acc2, acc1), 4, 0)
    last = acc1 + pltpu.roll(acc2, 4, 0)
    return first, last


def split(x):
    top = x.astype(BF16).astype(F32)
    return top, x - top


def vertex_rows(first, last, row):
    f0, f1 = split(first)
    l0, l1 = split(last)
    near = row < 3
    a0 = jnp.where(near, f0, pltpu.roll(f1, 3, 0))
    a1 = jnp.where(near, pltpu.roll(f0, 5, 0), f1)
    fl0 = jnp.where(row < 1, l0, f0)
    fl1 = jnp.where(row < 1, l1, f1)
    a2 = jnp.where(near, pltpu.roll(fl0, 2, 0), pltpu.roll(fl1, 5, 0))
    a3 = jnp.where(near, pltpu.roll(l0, 7, 0), pltpu.roll(l1, 2, 0))
    return a0, a1, a2, a3


def place(y8, block, count, rows):
    parts = [jnp.where(block == h, y8, 0.0) for h in range(count)]
    if rows > 8 * count:
        parts.append(jnp.zeros((rows - 8 * count, LANES), F32))
    return jnp.concatenate(parts, axis=0).astype(BF16)


def gather_sum(placed, hot):
    return jnp.dot(placed, hot, preferred_element_type=F32)


def kernel(
    right_hbm, mass_hbm, precond_hbm, ehess_hbm, enodes_hbm, halo_hbm, chess_hbm, point_hbm, slot_hbm,
    live_hbm, list_hbm, count_hbm,
    out_ref,
    right, mass, precond, ehess, enodes, halo, chess, point, slot, live, lists, count,
    ids, hot, ztab, own_tab, got_tab, zelem, zpoint, vert, total,
    yelem, ypoint, yslot, send_v, recv_v, send_r, recv_r, send_h, recv_h, sum_send, sum_a, sum_b,
    in_sem, sv_sem, rv_sem, sr_sem, rr_sem, sh_sem, rh_sem, ss_sem, ra_sem, rb_sem,
):
    region, sub = lax.axis_index("region"), lax.axis_index("sub")
    part = region * 8 + sub

    known = {}

    def device(offset):
        offset %= 128
        if offset not in known:
            q = lax.rem(part + offset, 128)
            known[offset] = (lax.div(q, 8), lax.rem(q, 8))
        return known[offset]

    def sub_peer(j):
        return (region, lax.rem(sub + j, 8))

    def region_peer(j):
        return (lax.rem(region + j, 16), sub)

    barrier = pltpu.get_barrier_semaphore()
    greeted = [device(o) for o in OFFSETS[1:]] + [sub_peer(j) for j in range(1, 8)]
    greeted += [region_peer(j) for j in range(1, 16) if j != 8]
    for peer in greeted:
        pl.semaphore_signal(barrier, inc=1, device_id=peer, device_id_type=MESH)

    pairs = [
        (right_hbm, right), (precond_hbm, precond), (list_hbm, lists), (count_hbm, count), (halo_hbm, halo),
        (mass_hbm, mass), (enodes_hbm, enodes), (point_hbm, point), (slot_hbm, slot), (live_hbm, live),
        (chess_hbm, chess), (ehess_hbm, ehess),
    ]
    copies = [pltpu.make_async_copy(src, dst, in_sem.at[i]) for i, (src, dst) in enumerate(pairs)]
    for copy in copies:
        copy.start()

    row = lax.broadcasted_iota(jnp.int32, (8, LANES), 0)
    lane = lax.broadcasted_iota(jnp.int32, (8, LANES), 1)

    for copy in copies[:6]:
        copy.wait()
    for m in range(3):
        for j in range(8):
            vert[m, j : j + 1, :] = right[m : m + 1, j * LANES : (j + 1) * LANES]
    for k in range(9):
        for j in range(8):
            vert[3 + k, j : j + 1, :] = precond[k : k + 1, j * LANES : (j + 1) * LANES]

    def precondition(vec):
        return [sum(vert[3 + 3 * m + l] * vec[l] for l in range(3)) for m in range(3)]

    ids[LIST_ROW : LIST_ROW + PEERS, :] = lists[:, 0, :]
    ids[LIST_ROW + PEERS : LIST_ROW + PEERS + 1, :] = jnp.concatenate([halo[1:2, :], halo[0:1, :]], axis=1)
    ids[LIST_ROW + PEERS + 1 : ID_ROWS, :] = jnp.zeros((ID_ROWS - LIST_ROW - PEERS - 1, LANES), jnp.int32)
    diag = lax.broadcasted_iota(jnp.int32, (16, PEERS), 0) == lax.broadcasted_iota(jnp.int32, (16, PEERS), 1)
    limit = jnp.sum(jnp.where(diag, jnp.broadcast_to(count[...], (16, PEERS)), 0).astype(F32), axis=1, keepdims=True)
    wide_row = lax.broadcasted_iota(jnp.int32, (16, LANES), 0)
    wide_lane = lax.broadcasted_iota(jnp.int32, (16, LANES), 1).astype(F32)
    list_live = jnp.where((wide_lane < limit) | (wide_row == HALO_ROW), 1.0, 0.0)

    def fill_own(vec):
        for m in range(3):
            for h in range(NODE_BLOCKS):
                own_tab[m, h] = spread(vec[m][h : h + 1, :])

    own_tables = [[own_tab.at[m, h] for h in range(NODE_BLOCKS)] for m in range(3)]
    got_tables = [[got_tab.at[m, k] for k in range(PEERS)] for m in range(3)]

    def read(tables):
        return [[t[...] for t in line] for line in tables]

    def offer(turn):
        got = [[], [], []]
        for g in range(2):
            found = pick(read(own_tables), ids[LIST_ROW + 8 * g : LIST_ROW + 8 * g + 8, :])
            for m in range(3):
                got[m].append(found[m] * list_live[8 * g : 8 * g + 8, :])
        for k in range(PEERS):
            for m in range(3):
                send_v[turn, k, m : m + 1, :] = got[m][k // 8][k % 8 : k % 8 + 1, :]
        for k in (UP, DOWN):
            for m in range(3):
                h = HALO_ROW
                send_v[turn, k, 3 + m : 4 + m, :] = got[m][h // 8][h % 8 : h % 8 + 1, :]

    def exchange(src, dst, s_sem, r_sem, turn, sign):
        return [
            pltpu.make_async_remote_copy(
                src_ref=src.at[turn, k], dst_ref=dst.at[turn, k], send_sem=s_sem.at[turn, k],
                recv_sem=r_sem.at[turn, k], device_id=device(sign * OFFSETS[k]), device_id_type=MESH,
            )
            for k in range(1, PEERS)
        ]

    started = []

    def own_lookups():
        def elem_group(g, carry):
            rows = pl.ds(pl.multiple_of(g * 8, 8), 8)
            found = pick(read(own_tables), ids[rows, :])
            for m in range(3):
                zelem[m, rows, :] = found[m]
            return carry

        lax.fori_loop(0, 16, elem_group, 0)
        for g in range(2):
            found = pick(read(own_tables), ids[POINT_ROW + 8 * g : POINT_ROW + 8 * g + 8, :])
            for m in range(3):
                zpoint[m, 8 * g : 8 * g + 8, :] = found[m]

    def energy(first, last, z):
        low = z[0]
        for c in range(1, 8):
            low = jnp.where(row == c, z[c], low)
        high = jnp.zeros((8, LANES), F32)
        for c in range(4):
            high = jnp.where(row == c, z[8 + c], high)
        return first * low + last * high

    def element_products(turn):
        rim = [
            jnp.where(lane < 64, spread(recv_v[turn, UP, 3 + m : 4 + m, :]), spread(recv_v[turn, DOWN, 3 + m : 4 + m, :]))
            for m in range(3)
        ]
        power = jnp.zeros((8, LANES), F32)
        for pair in range(ELEM_CHUNKS // 2):
            here = ids[8 * pair : 8 * pair + 8, :]
            hit = (here >> 7) == NODE_BLOCKS
            z8 = []
            for m in range(3):
                value = jnp.take_along_axis(rim[m], here & 127, axis=1, mode="promise_in_bounds")
                z8.append(jnp.where(hit, value, zelem[m, 8 * pair : 8 * pair + 8, :]))
            for half in range(2):
                chunk = 2 * pair + half
                z = [spread(z8[m][half * 4 + a : half * 4 + a + 1, :]) for a in range(4) for m in range(3)]
                first, last = block_product(ehess, chunk * LANES, z, row)
                power = power + energy(first, last, z)
                for a, y8 in enumerate(vertex_rows(first, last, row)):
                    yelem[chunk * 4 + a] = y8
        return power

    def contact_products(turn):
        for k in range(PEERS):
            for m in range(3):
                got_tab[m, k] = spread(recv_v[turn, k, m : m + 1, :])

        power = jnp.zeros((8, LANES), F32)
        for c in range(PAIR_CHUNKS // 8):
            zp = [zpoint[m, 8 * c : 8 * c + 8, :] for m in range(3)]
            alive = live[8 * c : 8 * c + 8, :].astype(F32)
            first_slot = SLOT_ROW + 24 * c
            zs = [pick(read(got_tables), ids[first_slot + 8 * i : first_slot + 8 * i + 8, :]) for i in range(3)]
            for q in range(8):
                chunk = c * 8 + q
                z = [spread(zp[m][q : q + 1, :]) for m in range(3)]
                where = [(3 * q + a) for a in range(3)]
                z += [spread(zs[w // 8][m][w % 8 : w % 8 + 1, :]) for w in where for m in range(3)]
                first, last = block_product(chess, chunk * LANES, z, row)
                gate = spread(alive[q : q + 1, :])
                first, last = first * gate, last * gate
                power = power + energy(first, last, z)
                ys = vertex_rows(first, last, row)
                ypoint[chunk] = ys[0]
                for a in range(3):
                    yslot[chunk * 3 + a] = ys[1 + a]
        return power

    def scatter(held, base, blocks, rows):
        placed = []
        for u, y8 in enumerate(held):
            if u % 8 == 0:
                block8 = ids[base + u : base + u + 8, :] >> 7
            placed.append(place(y8, spread(block8[u % 8 : u % 8 + 1, :]), blocks, rows))
        k0, k1 = base * LANES, (base + len(held)) * LANES
        return gather_sum(jnp.concatenate(placed, axis=1), hot[k0:k1, :])

    def finish(turn, acc, vec):
        placed = []
        for k in range(PEERS + 1):
            if k < PEERS:
                got = recv_r[turn, k] * spread(list_live[k : k + 1, :])
            else:
                got = jnp.where(lane < 64, recv_h[turn, 0], recv_h[turn, 1])
            top, rest = split(got)
            y8 = jnp.where(row < 3, top, pltpu.roll(rest, 3, 0))
            placed.append(y8)
        back = scatter(placed, LIST_ROW, NODE_BLOCKS, 64)
        total[...] = acc[:64] + back
        return [
            mass[...] * vec[m] + (total[pl.ds(m, 8, stride=8), :] + total[pl.ds(m + 3, 8, stride=8), :])
            for m in range(3)
        ]

    def send_values(turn, vec):
        fill_own(vec)
        offer(turn)

    def rows_of(values):
        out = jnp.zeros((8, LANES), F32)
        for i, value in enumerate(values):
            out = jnp.where(row == i, jnp.sum(value, axis=0, keepdims=True), out)
        return out

    def dot(a, b):
        return a[0] * b[0] + a[1] * b[1] + a[2] * b[2]

    def start_sub(turn, mine):
        sum_send[turn, 0] = mine
        out = [
            pltpu.make_async_remote_copy(
                src_ref=sum_send.at[turn, 0], dst_ref=sum_a.at[turn, j - 1], send_sem=ss_sem.at[turn, j - 1],
                recv_sem=ra_sem.at[turn, j - 1], device_id=sub_peer(j), device_id_type=MESH,
            )
            for j in range(1, 8)
        ]
        for copy in out:
            copy.start()
        return out

    def start_region(turn, first):
        for copy in first:
            copy.wait_recv()
        sum_send[turn, 1] = sum_send[turn, 0] + sum(sum_a[turn, j] for j in range(7))
        out = [
            pltpu.make_async_remote_copy(
                src_ref=sum_send.at[turn, 1], dst_ref=sum_b.at[turn, j - 1], send_sem=ss_sem.at[turn, 6 + j],
                recv_sem=rb_sem.at[turn, j - 1], device_id=region_peer(j), device_id_type=MESH,
            )
            for j in range(1, 16)
        ]
        for copy in out:
            copy.start()
        return out

    def end_sums(turn, second):
        for copy in second:
            copy.wait_recv()
        whole = sum_send[turn, 1] + sum(sum_b[turn, j] for j in range(15))
        whole = jnp.sum(whole, axis=1, keepdims=True)
        return [whole[i : i + 1, :] for i in range(3)]

    def operate(turn, vec, early, late, sums):
        copies = exchange(send_v, recv_v, sv_sem, rv_sem, turn, 1)
        for copy in copies:
            copy.start()
        started.extend(copies)
        early()
        own_lookups()
        recv_v[turn, 0] = send_v[turn, 0]
        for k in (UP, DOWN):
            copies[k - 1].wait_recv()
        power = element_products(turn)
        for k in range(1, PEERS):
            if k not in (UP, DOWN):
                copies[k - 1].wait_recv()
        power = power + contact_products(turn)
        power = power + mass[...] * dot(vec, vec)
        sub_copies = start_sub(turn, rows_of([power] + sums))

        acc_slot = scatter([yslot[u] for u in range(3 * PAIR_CHUNKS)], SLOT_ROW, PEERS, 8 * PEERS)
        for k in range(PEERS):
            out = acc_slot[8 * k : 8 * k + 8]
            out = out + pltpu.roll(out, 5, 0)
            if k == 0:
                recv_r[turn, 0] = out
            else:
                send_r[turn, k] = out
        back = exchange(send_r, recv_r, sr_sem, rr_sem, turn, -1)
        for copy in back:
            copy.start()
        own_rows = [yelem[u] for u in range(4 * ELEM_CHUNKS)] + [ypoint[u] for u in range(PAIR_CHUNKS)]
        acc = scatter(own_rows, ELEM_ROW, 9, OWN_ROWS)
        rim = acc[64:72]
        send_h[turn] = rim + pltpu.roll(rim, 5, 0)
        rims = [
            pltpu.make_async_remote_copy(
                src_ref=send_h.at[turn], dst_ref=recv_h.at[turn, i], send_sem=sh_sem.at[turn, i],
                recv_sem=rh_sem.at[turn, i], device_id=device(-OFFSETS[k]), device_id_type=MESH,
            )
            for i, k in enumerate((UP, DOWN))
        ]
        for copy in rims:
            copy.start()
        late()
        region_copies = start_region(turn, sub_copies)
        for copy in rims + back:
            copy.wait_recv()
        image = finish(turn, acc, vec)
        started.extend(rims + back + sub_copies + region_copies)
        return image, end_sums(turn, region_copies)

    rhs = [vert[m] for m in range(3)]
    d0 = precondition(rhs)
    send_values(0, d0)

    tall = lax.broadcasted_iota(jnp.int32, (LANES, LANES), 0)

    def hot_rows(first, last):
        def group(g, carry):
            low8 = ids[pl.ds(pl.multiple_of(g * 8, 8), 8), :] & 127
            for q in range(8):
                hit = jnp.broadcast_to(low8[q : q + 1, :], (LANES, LANES)) == tall
                k0 = pl.multiple_of((g * 8 + q) * LANES, LANES)
                hot[pl.ds(k0, LANES), :] = jnp.where(hit, 1.0, 0.0).astype(BF16).T
            return carry

        lax.fori_loop(first, last, group, 0)

    def prepare():
        for copy in copies[6:10]:
            copy.wait()
        for chunk in range(ELEM_CHUNKS):
            ids[4 * chunk : 4 * chunk + 4, :] = enodes[:, chunk * LANES : (chunk + 1) * LANES]
        ids[POINT_ROW : POINT_ROW + PAIR_CHUNKS, :] = point[...]
        for chunk in range(PAIR_CHUNKS):
            ids[SLOT_ROW + 3 * chunk : SLOT_ROW + 3 * chunk + 3, :] = slot[:, chunk * LANES : (chunk + 1) * LANES]

        hot_rows(0, LIST_ROW // 8)
        for copy in copies[10:]:
            copy.wait()

    pl.semaphore_wait(barrier, len(greeted))
    u0, (curve0, gamma0, _) = operate(0, d0, prepare, lambda: hot_rows(LIST_ROW // 8, ID_ROWS // 8), [dot(rhs, d0)])
    alpha = gamma0 / curve0
    r1 = [rhs[m] - alpha * u0[m] for m in range(3)]
    s1 = precondition(r1)
    send_values(1, s1)
    a1, (same, gamma1, cross) = operate(1, s1, lambda: None, lambda: None, [dot(r1, s1), dot(s1, u0)])
    beta = gamma1 / gamma0
    curve1 = same + 2.0 * beta * cross + beta * beta * curve0
    alpha1 = gamma1 / curve1
    for m in range(3):
        d1 = s1[m] + beta * d0[m]
        image = a1[m] + beta * u0[m]
        out_s = alpha * d0[m] + alpha1 * d1
        out_r = r1[m] - alpha1 * image
        for j in range(8):
            out_ref[m : m + 1, j * LANES : (j + 1) * LANES] = out_s[j : j + 1, :]
            out_ref[3 + m : 4 + m, j * LANES : (j + 1) * LANES] = out_r[j : j + 1, :]
    for copy in started:
        copy.wait_send()


def per_device(
    right_side, node_mass, precond, elem_hess, elem_nodes, halo_lists, contact_hess, pair_point, pair_slot,
    pair_live, contact_send, send_counts,
):
    any_space = pl.BlockSpec(memory_space=pl.ANY)
    vmem = pl.BlockSpec(memory_space=pltpu.VMEM)
    args = (
        right_side, node_mass.reshape(8, LANES), precond, elem_hess, elem_nodes, halo_lists, contact_hess,
        pair_point.reshape(-1, LANES), pair_slot, pair_live.reshape(-1, LANES), contact_send.swapaxes(0, 1), send_counts,
    )
    out = jax.ShapeDtypeStruct((6, right_side.shape[1]), F32)
    dma = pltpu.SemaphoreType.DMA
    both = pl.pallas_call(
        kernel,
        out_shape=out,
        in_specs=[any_space] * len(args),
        out_specs=vmem,
        scratch_shapes=[pltpu.VMEM(a.shape, a.dtype) for a in args]
        + [
            pltpu.VMEM((ID_ROWS, LANES), jnp.int32),
            pltpu.VMEM((ID_ROWS * LANES, LANES), BF16),
            pltpu.VMEM((3, 8, LANES), F32),
            pltpu.VMEM((3, NODE_BLOCKS, 8, LANES), F32),
            pltpu.VMEM((3, PEERS, 8, LANES), F32),
            pltpu.VMEM((3, 4 * ELEM_CHUNKS, LANES), F32),
            pltpu.VMEM((3, PAIR_CHUNKS, LANES), F32),
            pltpu.VMEM((12, 8, LANES), F32),
            pltpu.VMEM((64, LANES), F32),
            pltpu.VMEM((4 * ELEM_CHUNKS, 8, LANES), F32),
            pltpu.VMEM((PAIR_CHUNKS, 8, LANES), F32),
            pltpu.VMEM((3 * PAIR_CHUNKS, 8, LANES), F32),
            pltpu.VMEM((2, PEERS, 8, LANES), F32),
            pltpu.VMEM((2, PEERS, 8, LANES), F32),
            pltpu.VMEM((2, PEERS, 8, LANES), F32),
            pltpu.VMEM((2, PEERS, 8, LANES), F32),
            pltpu.VMEM((2, 8, LANES), F32),
            pltpu.VMEM((2, 2, 8, LANES), F32),
            pltpu.VMEM((2, 2, 8, LANES), F32),
            pltpu.VMEM((2, 7, 8, LANES), F32),
            pltpu.VMEM((2, 15, 8, LANES), F32),
            dma((len(args),)),
            dma((2, PEERS)),
            dma((2, PEERS)),
            dma((2, PEERS)),
            dma((2, PEERS)),
            dma((2, 2)),
            dma((2, 2)),
            dma((2, 22)),
            dma((2, 7)),
            dma((2, 15)),
        ],
        compiler_params=pltpu.CompilerParams(
            collective_id=0, has_side_effects=True, vmem_limit_bytes=60 * 1024 * 1024
        ),
    )(*args)
    return both[:3], both[3:]


def solution(mesh):
    both = P(None, AXES)
    return jax.shard_map(
        per_device,
        mesh=mesh,
        in_specs=(
            both, P(AXES), both, both, both, both, both, P(AXES), both, P(AXES), P(AXES, None, None), P(AXES, None),
        ),
        out_specs=(both, both),
        check_vma=False,
    )
```

```python
import jax
import jax.numpy as jnp
from jax import lax
from jax.experimental import pallas as pl
from jax.experimental.pallas import tpu as pltpu
from jax.sharding import PartitionSpec as P

MESH = pl.DeviceIdType.MESH
AXES = ("region", "sub")
F32 = jnp.float32
BF16 = jnp.bfloat16
LANES = 128
OFFSETS = (0, 1, 2, 3, 4, -1, -2, -3, -4, 64, 65, 63)
PEERS = len(OFFSETS)
UP, DOWN = 1, 5
NODE_BLOCKS = 8
ELEM_CHUNKS = 32
PAIR_CHUNKS = 16
ELEM_ROW, POINT_ROW, SLOT_ROW, LIST_ROW, ID_ROWS = 0, 128, 144, 192, 208
HALO_ROW = PEERS
OWN_ROWS = 80


def spread(row):
    return jnp.broadcast_to(row, (8, LANES))


def pick(tables, ids):
    block, lane = ids >> 7, ids & 127
    found = [jnp.zeros(ids.shape, F32) for _ in range(3)]
    for h in range(len(tables[0])):
        hit = block == h
        for m in range(3):
            value = jnp.take_along_axis(tables[m][h], lane, axis=1, mode="promise_in_bounds")
            found[m] = jnp.where(hit, value, found[m])
    return found


def block_product(hess, start, z, row):
    lanes = pl.ds(start, LANES)
    low = row < 4
    acc0 = acc1 = acc2 = None
    for j in range(6):
        za, zb = z[2 * j], z[2 * j + 1]
        t0 = hess[24 * j : 24 * j + 8, lanes] * za
        t1 = hess[24 * j + 8 : 24 * j + 16, lanes] * jnp.where(low, za, zb)
        t2 = hess[24 * j + 16 : 24 * j + 24, lanes] * zb
        if j == 0:
            acc0, acc1, acc2 = t0, t1, t2
        else:
            acc0, acc1, acc2 = acc0 + t0, acc1 + t1, acc2 + t2
    first = acc0 + pltpu.roll(jnp.where(low, acc2, acc1), 4, 0)
    last = acc1 + pltpu.roll(acc2, 4, 0)
    return first, last


def split(x):
    top = x.astype(BF16).astype(F32)
    return top, x - top


def vertex_rows(first, last, row):
    f0, f1 = split(first)
    l0, l1 = split(last)
    near = row < 3
    a0 = jnp.where(near, f0, pltpu.roll(f1, 3, 0))
    a1 = jnp.where(near, pltpu.roll(f0, 5, 0), f1)
    fl0 = jnp.where(row < 1, l0, f0)
    fl1 = jnp.where(row < 1, l1, f1)
    a2 = jnp.where(near, pltpu.roll(fl0, 2, 0), pltpu.roll(fl1, 5, 0))
    a3 = jnp.where(near, pltpu.roll(l0, 7, 0), pltpu.roll(l1, 2, 0))
    return a0, a1, a2, a3


def place(y8, block, count, rows):
    parts = [jnp.where(block == h, y8, 0.0) for h in range(count)]
    if rows > 8 * count:
        parts.append(jnp.zeros((rows - 8 * count, LANES), F32))
    return jnp.concatenate(parts, axis=0).astype(BF16)


def gather_sum(placed, hot):
    return jnp.dot(placed, hot, preferred_element_type=F32)


def kernel(
    right_hbm, mass_hbm, precond_hbm, ehess_hbm, enodes_hbm, halo_hbm, chess_hbm, point_hbm, slot_hbm,
    live_hbm, list_hbm, count_hbm,
    out_ref,
    right, mass, precond, ehess, enodes, halo, chess, point, slot, live, lists, count,
    ids, hot, ztab, own_tab, got_tab, zelem, zpoint, vert, total,
    yelem, ypoint, yslot, send_v, step_v, recv_v, send_r, recv_r, send_h, recv_h, sum_send, sum_a, sum_b,
    in_sem, sv_sem, rv_sem, sr_sem, rr_sem, sh_sem, rh_sem, ss_sem, ra_sem, rb_sem,
):
    region, sub = lax.axis_index("region"), lax.axis_index("sub")
    part = region * 8 + sub

    known = {}

    def device(offset):
        offset %= 128
        if offset not in known:
            q = lax.rem(part + offset, 128)
            known[offset] = (lax.div(q, 8), lax.rem(q, 8))
        return known[offset]

    def sub_peer(j):
        return (region, lax.rem(sub + j, 8))

    def region_peer(j):
        return (lax.rem(region + j, 16), sub)

    barrier = pltpu.get_barrier_semaphore()
    greeted = [device(o) for o in OFFSETS[1:]] + [sub_peer(j) for j in range(1, 8)]
    greeted += [region_peer(j) for j in range(1, 16) if j != 8]
    for peer in greeted:
        pl.semaphore_signal(barrier, inc=1, device_id=peer, device_id_type=MESH)

    pairs = [
        (right_hbm, right), (precond_hbm, precond), (list_hbm, lists), (count_hbm, count), (halo_hbm, halo),
        (mass_hbm, mass), (enodes_hbm, enodes), (point_hbm, point), (slot_hbm, slot), (live_hbm, live),
        (chess_hbm, chess), (ehess_hbm, ehess),
    ]
    copies = [pltpu.make_async_copy(src, dst, in_sem.at[i]) for i, (src, dst) in enumerate(pairs)]
    for copy in copies:
        copy.start()

    row = lax.broadcasted_iota(jnp.int32, (8, LANES), 0)
    lane = lax.broadcasted_iota(jnp.int32, (8, LANES), 1)

    for copy in copies[:6]:
        copy.wait()
    for m in range(3):
        for j in range(8):
            vert[m, j : j + 1, :] = right[m : m + 1, j * LANES : (j + 1) * LANES]
    for k in range(9):
        for j in range(8):
            vert[3 + k, j : j + 1, :] = precond[k : k + 1, j * LANES : (j + 1) * LANES]

    def precondition(vec):
        return [sum(vert[3 + 3 * m + l] * vec[l] for l in range(3)) for m in range(3)]

    ids[LIST_ROW : LIST_ROW + PEERS, :] = lists[:, 0, :]
    ids[LIST_ROW + PEERS : LIST_ROW + PEERS + 1, :] = jnp.concatenate([halo[1:2, :], halo[0:1, :]], axis=1)
    ids[LIST_ROW + PEERS + 1 : ID_ROWS, :] = jnp.zeros((ID_ROWS - LIST_ROW - PEERS - 1, LANES), jnp.int32)
    diag = lax.broadcasted_iota(jnp.int32, (16, PEERS), 0) == lax.broadcasted_iota(jnp.int32, (16, PEERS), 1)
    limit = jnp.sum(jnp.where(diag, jnp.broadcast_to(count[...], (16, PEERS)), 0).astype(F32), axis=1, keepdims=True)
    wide_row = lax.broadcasted_iota(jnp.int32, (16, LANES), 0)
    wide_lane = lax.broadcasted_iota(jnp.int32, (16, LANES), 1).astype(F32)
    list_live = jnp.where((wide_lane < limit) | (wide_row == HALO_ROW), 1.0, 0.0)

    def fill_own(vec):
        for m in range(3):
            for h in range(NODE_BLOCKS):
                own_tab[m, h] = spread(vec[m][h : h + 1, :])

    own_tables = [[own_tab.at[m, h] for h in range(NODE_BLOCKS)] for m in range(3)]
    got_tables = [[got_tab.at[m, k] for k in range(PEERS)] for m in range(3)]

    def read(tables):
        return [[t[...] for t in line] for line in tables]

    def offer(kept):
        got = [[], [], []]
        for g in range(2):
            found = pick(read(own_tables), ids[LIST_ROW + 8 * g : LIST_ROW + 8 * g + 8, :])
            for m in range(3):
                got[m].append(found[m] * list_live[8 * g : 8 * g + 8, :])
        for k in range(PEERS):
            for m in range(3):
                kept[k, m : m + 1, :] = got[m][k // 8][k % 8 : k % 8 + 1, :]
        for k in (UP, DOWN):
            for m in range(3):
                h = HALO_ROW
                kept[k, 3 + m : 4 + m, :] = got[m][h // 8][h % 8 : h % 8 + 1, :]

    def used(k, sign):
        return pl.ds(0, 6 if sign > 0 and k in (UP, DOWN) else 3)

    def exchange(src, dst, s_sem, r_sem, turn, sign):
        return [
            pltpu.make_async_remote_copy(
                src_ref=src.at[turn, k, used(k, sign)], dst_ref=dst.at[turn, k, used(k, sign)], send_sem=s_sem.at[turn, k],
                recv_sem=r_sem.at[turn, k], device_id=device(sign * OFFSETS[k]), device_id_type=MESH,
            )
            for k in range(1, PEERS)
        ]

    started = []

    def own_lookups():
        def elem_group(g, carry):
            rows = pl.ds(pl.multiple_of(g * 8, 8), 8)
            found = pick(read(own_tables), ids[rows, :])
            for m in range(3):
                zelem[m, rows, :] = found[m]
            return carry

        lax.fori_loop(0, 16, elem_group, 0)
        for g in range(2):
            found = pick(read(own_tables), ids[POINT_ROW + 8 * g : POINT_ROW + 8 * g + 8, :])
            for m in range(3):
                zpoint[m, 8 * g : 8 * g + 8, :] = found[m]

    def energy(first, last, z):
        low = z[0]
        for c in range(1, 8):
            low = jnp.where(row == c, z[c], low)
        high = jnp.zeros((8, LANES), F32)
        for c in range(4):
            high = jnp.where(row == c, z[8 + c], high)
        return first * low + last * high

    def element_products(turn):
        rim = [
            jnp.where(lane < 64, spread(recv_v[turn, UP, 3 + m : 4 + m, :]), spread(recv_v[turn, DOWN, 3 + m : 4 + m, :]))
            for m in range(3)
        ]
        power = jnp.zeros((8, LANES), F32)
        for pair in range(ELEM_CHUNKS // 2):
            here = ids[8 * pair : 8 * pair + 8, :]
            hit = (here >> 7) == NODE_BLOCKS
            z8 = []
            for m in range(3):
                value = jnp.take_along_axis(rim[m], here & 127, axis=1, mode="promise_in_bounds")
                z8.append(jnp.where(hit, value, zelem[m, 8 * pair : 8 * pair + 8, :]))
            for half in range(2):
                chunk = 2 * pair + half
                z = [spread(z8[m][half * 4 + a : half * 4 + a + 1, :]) for a in range(4) for m in range(3)]
                first, last = block_product(ehess, chunk * LANES, z, row)
                power = power + energy(first, last, z)
                for a, y8 in enumerate(vertex_rows(first, last, row)):
                    yelem[chunk * 4 + a] = y8
        return power

    def contact_products(turn):
        for k in range(PEERS):
            for m in range(3):
                got_tab[m, k] = spread(recv_v[turn, k, m : m + 1, :])

        power = jnp.zeros((8, LANES), F32)
        for c in range(PAIR_CHUNKS // 8):
            zp = [zpoint[m, 8 * c : 8 * c + 8, :] for m in range(3)]
            alive = live[8 * c : 8 * c + 8, :].astype(F32)
            first_slot = SLOT_ROW + 24 * c
            zs = [pick(read(got_tables), ids[first_slot + 8 * i : first_slot + 8 * i + 8, :]) for i in range(3)]
            for q in range(8):
                chunk = c * 8 + q
                z = [spread(zp[m][q : q + 1, :]) for m in range(3)]
                where = [(3 * q + a) for a in range(3)]
                z += [spread(zs[w // 8][m][w % 8 : w % 8 + 1, :]) for w in where for m in range(3)]
                first, last = block_product(chess, chunk * LANES, z, row)
                gate = spread(alive[q : q + 1, :])
                first, last = first * gate, last * gate
                power = power + energy(first, last, z)
                ys = vertex_rows(first, last, row)
                ypoint[chunk] = ys[0]
                for a in range(3):
                    yslot[chunk * 3 + a] = ys[1 + a]
        return power

    def scatter(held, base, blocks, rows):
        placed = []
        for u, y8 in enumerate(held):
            if u % 8 == 0:
                block8 = ids[base + u : base + u + 8, :] >> 7
            placed.append(place(y8, spread(block8[u % 8 : u % 8 + 1, :]), blocks, rows))
        k0, k1 = base * LANES, (base + len(held)) * LANES
        return gather_sum(jnp.concatenate(placed, axis=1), hot[k0:k1, :])

    def finish(turn, acc, vec):
        placed = []
        for k in range(PEERS + 1):
            if k < PEERS:
                got = recv_r[turn, k] * spread(list_live[k : k + 1, :])
            else:
                got = jnp.where(lane < 64, recv_h[turn, 0], recv_h[turn, 1])
            top, rest = split(got)
            y8 = jnp.where(row < 3, top, pltpu.roll(rest, 3, 0))
            placed.append(y8)
        back = scatter(placed, LIST_ROW, NODE_BLOCKS, 64)
        total[...] = acc[:64] + back
        return [
            mass[...] * vec[m] + (total[pl.ds(m, 8, stride=8), :] + total[pl.ds(m + 3, 8, stride=8), :])
            for m in range(3)
        ]

    def rows_of(values):
        out = jnp.zeros((8, LANES), F32)
        for i, value in enumerate(values):
            out = jnp.where(row == i, jnp.sum(value, axis=0, keepdims=True), out)
        return out

    def dot(a, b):
        return a[0] * b[0] + a[1] * b[1] + a[2] * b[2]

    def start_sub(turn, mine):
        sum_send[turn, 0] = mine
        out = [
            pltpu.make_async_remote_copy(
                src_ref=sum_send.at[turn, 0, pl.ds(0, 3)], dst_ref=sum_a.at[turn, j - 1, pl.ds(0, 3)], send_sem=ss_sem.at[turn, j - 1],
                recv_sem=ra_sem.at[turn, j - 1], device_id=sub_peer(j), device_id_type=MESH,
            )
            for j in range(1, 8)
        ]
        for copy in out:
            copy.start()
        return out

    def start_region(turn, first):
        for copy in first:
            copy.wait_recv()
        sum_send[turn, 1] = sum_send[turn, 0] + sum(sum_a[turn, j] for j in range(7))
        out = [
            pltpu.make_async_remote_copy(
                src_ref=sum_send.at[turn, 1, pl.ds(0, 3)], dst_ref=sum_b.at[turn, j - 1, pl.ds(0, 3)], send_sem=ss_sem.at[turn, 6 + j],
                recv_sem=rb_sem.at[turn, j - 1], device_id=region_peer(j), device_id_type=MESH,
            )
            for j in range(1, 16)
        ]
        for copy in out:
            copy.start()
        return out

    def end_sums(turn, second):
        for copy in second:
            copy.wait_recv()
        whole = sum_send[turn, 1] + sum(sum_b[turn, j] for j in range(15))
        whole = jnp.sum(whole, axis=1, keepdims=True)
        return [whole[i : i + 1, :] for i in range(3)]

    def operate(turn, vec, copies, early, late, sums):
        started.extend(copies)
        early()
        own_lookups()
        recv_v[turn, 0] = send_v[turn, 0]
        for k in (UP, DOWN):
            copies[k - 1].wait_recv()
        power = element_products(turn)
        for k in range(1, PEERS):
            if k not in (UP, DOWN):
                copies[k - 1].wait_recv()
        power = power + contact_products(turn)
        power = power + mass[...] * dot(vec, vec)
        sub_copies = start_sub(turn, rows_of([power] + sums))

        acc_slot = scatter([yslot[u] for u in range(3 * PAIR_CHUNKS)], SLOT_ROW, PEERS, 8 * PEERS)
        for k in range(PEERS):
            out = acc_slot[8 * k : 8 * k + 8]
            out = out + pltpu.roll(out, 5, 0)
            if k == 0:
                recv_r[turn, 0] = out
            else:
                send_r[turn, k] = out
        back = exchange(send_r, recv_r, sr_sem, rr_sem, turn, -1)
        for copy in back:
            copy.start()
        own_rows = [yelem[u] for u in range(4 * ELEM_CHUNKS)] + [ypoint[u] for u in range(PAIR_CHUNKS)]
        acc = scatter(own_rows, ELEM_ROW, 9, OWN_ROWS)
        rim = acc[64:72]
        send_h[turn] = rim + pltpu.roll(rim, 5, 0)
        rims = [
            pltpu.make_async_remote_copy(
                src_ref=send_h.at[turn, pl.ds(0, 3)], dst_ref=recv_h.at[turn, i, pl.ds(0, 3)], send_sem=sh_sem.at[turn, i],
                recv_sem=rh_sem.at[turn, i], device_id=device(-OFFSETS[k]), device_id_type=MESH,
            )
            for i, k in enumerate((UP, DOWN))
        ]
        for copy in rims:
            copy.start()
        late()
        region_copies = start_region(turn, sub_copies)
        started.extend(rims + back + sub_copies)
        if turn == 1:
            for copy in started:
                copy.wait_send()
        for copy in rims + back:
            copy.wait_recv()
        return finish(turn, acc, vec), region_copies

    rhs = [vert[m] for m in range(3)]
    d0 = precondition(rhs)
    fill_own(d0)
    offer(send_v.at[0])
    copies_v = exchange(send_v, recv_v, sv_sem, rv_sem, 0, 1)

    tall = lax.broadcasted_iota(jnp.int32, (LANES, LANES), 0)

    def hot_rows(first, last):
        def group(g, carry):
            low8 = ids[pl.ds(pl.multiple_of(g * 8, 8), 8), :] & 127
            for q in range(8):
                hit = jnp.broadcast_to(low8[q : q + 1, :], (LANES, LANES)) == tall
                k0 = pl.multiple_of((g * 8 + q) * LANES, LANES)
                hot[pl.ds(k0, LANES), :] = jnp.where(hit, 1.0, 0.0).astype(BF16).T
            return carry

        lax.fori_loop(first, last, group, 0)

    def prepare():
        for copy in copies[6:10]:
            copy.wait()
        for chunk in range(ELEM_CHUNKS):
            ids[4 * chunk : 4 * chunk + 4, :] = enodes[:, chunk * LANES : (chunk + 1) * LANES]
        ids[POINT_ROW : POINT_ROW + PAIR_CHUNKS, :] = point[...]
        for chunk in range(PAIR_CHUNKS):
            ids[SLOT_ROW + 3 * chunk : SLOT_ROW + 3 * chunk + 3, :] = slot[:, chunk * LANES : (chunk + 1) * LANES]

        hot_rows(0, LIST_ROW // 8)
        for copy in copies[10:]:
            copy.wait()

    pl.semaphore_wait(barrier, len(greeted))
    for copy in copies_v:
        copy.start()
    u0, region0 = operate(
        0, d0, copies_v, prepare, lambda: hot_rows(LIST_ROW // 8, ID_ROWS // 8), [dot(rhs, d0)]
    )

    largest = jnp.maximum(jnp.maximum(jnp.abs(u0[0]), jnp.abs(u0[1])), jnp.abs(u0[2]))
    largest = jnp.max(jnp.max(largest, axis=1, keepdims=True), axis=0, keepdims=True)
    largest = jnp.maximum(largest, 1e-30)
    unit = 1.0 / largest
    fill_own(precondition([u0[m] * unit for m in range(3)]))
    offer(step_v)
    curve0, gamma0, _ = end_sums(0, region0)
    alpha = gamma0 / curve0
    factor = spread(alpha * largest)
    copies_v = exchange(send_v, recv_v, sv_sem, rv_sem, 1, 1)
    for k in range(1, PEERS):
        send_v[1, k] = send_v[0, k] - factor * step_v[k]
        copies_v[k - 1].start()
    send_v[1, 0] = send_v[0, 0] - factor * step_v[0]
    r1 = [rhs[m] - alpha * u0[m] for m in range(3)]
    s1 = precondition(r1)
    fill_own(s1)
    a1, region1 = operate(1, s1, copies_v, lambda: None, lambda: None, [dot(r1, s1), dot(s1, u0)])
    for copy in region0 + region1:
        copy.wait_send()
    same, gamma1, cross = end_sums(1, region1)
    beta = gamma1 / gamma0
    curve1 = same + 2.0 * beta * cross + beta * beta * curve0
    alpha1 = gamma1 / curve1
    for m in range(3):
        d1 = s1[m] + beta * d0[m]
        image = a1[m] + beta * u0[m]
        out_s = alpha * d0[m] + alpha1 * d1
        out_r = r1[m] - alpha1 * image
        for j in range(8):
            out_ref[m : m + 1, j * LANES : (j + 1) * LANES] = out_s[j : j + 1, :]
            out_ref[3 + m : 4 + m, j * LANES : (j + 1) * LANES] = out_r[j : j + 1, :]


def per_device(
    right_side, node_mass, precond, elem_hess, elem_nodes, halo_lists, contact_hess, pair_point, pair_slot,
    pair_live, contact_send, send_counts,
):
    any_space = pl.BlockSpec(memory_space=pl.ANY)
    vmem = pl.BlockSpec(memory_space=pltpu.VMEM)
    args = (
        right_side, node_mass.reshape(8, LANES), precond, elem_hess, elem_nodes, halo_lists, contact_hess,
        pair_point.reshape(-1, LANES), pair_slot, pair_live.reshape(-1, LANES), contact_send.swapaxes(0, 1), send_counts,
    )
    out = jax.ShapeDtypeStruct((6, right_side.shape[1]), F32)
    dma = pltpu.SemaphoreType.DMA
    both = pl.pallas_call(
        kernel,
        out_shape=out,
        in_specs=[any_space] * len(args),
        out_specs=vmem,
        scratch_shapes=[pltpu.VMEM(a.shape, a.dtype) for a in args]
        + [
            pltpu.VMEM((ID_ROWS, LANES), jnp.int32),
            pltpu.VMEM((ID_ROWS * LANES, LANES), BF16),
            pltpu.VMEM((3, 8, LANES), F32),
            pltpu.VMEM((3, NODE_BLOCKS, 8, LANES), F32),
            pltpu.VMEM((3, PEERS, 8, LANES), F32),
            pltpu.VMEM((3, 4 * ELEM_CHUNKS, LANES), F32),
            pltpu.VMEM((3, PAIR_CHUNKS, LANES), F32),
            pltpu.VMEM((12, 8, LANES), F32),
            pltpu.VMEM((64, LANES), F32),
            pltpu.VMEM((4 * ELEM_CHUNKS, 8, LANES), F32),
            pltpu.VMEM((PAIR_CHUNKS, 8, LANES), F32),
            pltpu.VMEM((3 * PAIR_CHUNKS, 8, LANES), F32),
            pltpu.VMEM((2, PEERS, 8, LANES), F32),
            pltpu.VMEM((PEERS, 8, LANES), F32),
            pltpu.VMEM((2, PEERS, 8, LANES), F32),
            pltpu.VMEM((2, PEERS, 8, LANES), F32),
            pltpu.VMEM((2, PEERS, 8, LANES), F32),
            pltpu.VMEM((2, 8, LANES), F32),
            pltpu.VMEM((2, 2, 8, LANES), F32),
            pltpu.VMEM((2, 2, 8, LANES), F32),
            pltpu.VMEM((2, 7, 8, LANES), F32),
            pltpu.VMEM((2, 15, 8, LANES), F32),
            dma((len(args),)),
            dma((2, PEERS)),
            dma((2, PEERS)),
            dma((2, PEERS)),
            dma((2, PEERS)),
            dma((2, 2)),
            dma((2, 2)),
            dma((2, 22)),
            dma((2, 7)),
            dma((2, 15)),
        ],
        compiler_params=pltpu.CompilerParams(
            collective_id=0, has_side_effects=True, vmem_limit_bytes=60 * 1024 * 1024
        ),
    )(*args)
    return both[:3], both[3:]


def solution(mesh):
    both = P(None, AXES)
    return jax.shard_map(
        per_device,
        mesh=mesh,
        in_specs=(
            both, P(AXES), both, both, both, both, both, P(AXES), both, P(AXES), P(AXES, None, None), P(AXES, None),
        ),
        out_specs=(both, both),
        check_vma=False,
    )
```

```python
import jax
import jax.numpy as jnp
from jax import lax
from jax.experimental import pallas as pl
from jax.experimental.pallas import tpu as pltpu
from jax.sharding import PartitionSpec as P

MESH = pl.DeviceIdType.MESH
AXES = ("region", "sub")
F32 = jnp.float32
BF16 = jnp.bfloat16
LANES = 128
OFFSETS = (0, 1, 2, 3, 4, -1, -2, -3, -4, 64, 65, 63)
PEERS = len(OFFSETS)
FAR_FIRST = (10, 11, 4, 8, 3, 7, 9, 2, 6, 1, 5)
UP, DOWN = 1, 5
NODE_BLOCKS = 8
ELEM_CHUNKS = 32
PAIR_CHUNKS = 16
ELEM_ROW, POINT_ROW, SLOT_ROW, LIST_ROW, ID_ROWS = 0, 128, 144, 192, 208
HALO_ROW = PEERS
OWN_ROWS = 80


def spread(row):
    return jnp.broadcast_to(row, (8, LANES))


def pick(tables, ids):
    block, lane = ids >> 7, ids & 127
    found = [jnp.zeros(ids.shape, F32) for _ in range(3)]
    for h in range(len(tables[0])):
        hit = block == h
        for m in range(3):
            value = jnp.take_along_axis(tables[m][h], lane, axis=1, mode="promise_in_bounds")
            found[m] = jnp.where(hit, value, found[m])
    return found


def block_product(hess, start, z, row):
    lanes = pl.ds(start, LANES)
    low = row < 4
    acc0 = acc1 = acc2 = None
    for j in range(6):
        za, zb = z[2 * j], z[2 * j + 1]
        t0 = hess[24 * j : 24 * j + 8, lanes] * za
        t1 = hess[24 * j + 8 : 24 * j + 16, lanes] * jnp.where(low, za, zb)
        t2 = hess[24 * j + 16 : 24 * j + 24, lanes] * zb
        if j == 0:
            acc0, acc1, acc2 = t0, t1, t2
        else:
            acc0, acc1, acc2 = acc0 + t0, acc1 + t1, acc2 + t2
    first = acc0 + pltpu.roll(jnp.where(low, acc2, acc1), 4, 0)
    last = acc1 + pltpu.roll(acc2, 4, 0)
    return first, last


def split(x):
    top = x.astype(BF16).astype(F32)
    return top, x - top


def vertex_rows(first, last, row):
    f0, f1 = split(first)
    l0, l1 = split(last)
    near = row < 3
    a0 = jnp.where(near, f0, pltpu.roll(f1, 3, 0))
    a1 = jnp.where(near, pltpu.roll(f0, 5, 0), f1)
    fl0 = jnp.where(row < 1, l0, f0)
    fl1 = jnp.where(row < 1, l1, f1)
    a2 = jnp.where(near, pltpu.roll(fl0, 2, 0), pltpu.roll(fl1, 5, 0))
    a3 = jnp.where(near, pltpu.roll(l0, 7, 0), pltpu.roll(l1, 2, 0))
    return a0, a1, a2, a3


def place(y8, block, count, rows):
    parts = [jnp.where(block == h, y8, 0.0) for h in range(count)]
    if rows > 8 * count:
        parts.append(jnp.zeros((rows - 8 * count, LANES), F32))
    return jnp.concatenate(parts, axis=0).astype(BF16)


def gather_sum(placed, hot):
    return jnp.dot(placed, hot, preferred_element_type=F32)


def kernel(
    right_hbm, mass_hbm, precond_hbm, ehess_hbm, enodes_hbm, halo_hbm, chess_hbm, point_hbm, slot_hbm,
    live_hbm, list_hbm, count_hbm,
    out_ref,
    right, mass, precond, ehess, enodes, halo, chess, point, slot, live, lists, count,
    ids, hot, ztab, own_tab, got_tab, zelem, zpoint, vert, total,
    yelem, ypoint, yslot, send_v, step_v, recv_v, send_r, recv_r, send_h, recv_h, sum_send, sum_a, sum_b,
    in_sem, sv_sem, rv_sem, sr_sem, rr_sem, sh_sem, rh_sem, ss_sem, ra_sem, rb_sem,
):
    region, sub = lax.axis_index("region"), lax.axis_index("sub")
    part = region * 8 + sub

    known = {}

    def device(offset):
        offset %= 128
        if offset not in known:
            q = lax.rem(part + offset, 128)
            known[offset] = (lax.div(q, 8), lax.rem(q, 8))
        return known[offset]

    def sub_peer(j):
        return (region, lax.rem(sub + j, 8))

    def region_peer(j):
        return (lax.rem(region + j, 16), sub)

    pairs = [
        (right_hbm, right), (precond_hbm, precond), (list_hbm, lists), (count_hbm, count), (halo_hbm, halo),
        (mass_hbm, mass), (enodes_hbm, enodes), (point_hbm, point), (slot_hbm, slot), (live_hbm, live),
        (chess_hbm, chess), (ehess_hbm, ehess),
    ]
    copies = [pltpu.make_async_copy(src, dst, in_sem.at[i]) for i, (src, dst) in enumerate(pairs)]
    for copy in copies:
        copy.start()

    barrier = pltpu.get_barrier_semaphore()
    greeted = [device(o) for o in OFFSETS[1:]] + [sub_peer(j) for j in range(1, 8)]
    greeted += [region_peer(j) for j in range(1, 16) if j != 8]
    for peer in greeted:
        pl.semaphore_signal(barrier, inc=1, device_id=peer, device_id_type=MESH)

    row = lax.broadcasted_iota(jnp.int32, (8, LANES), 0)
    lane = lax.broadcasted_iota(jnp.int32, (8, LANES), 1)

    for copy in copies[:6]:
        copy.wait()
    for m in range(3):
        for j in range(8):
            vert[m, j : j + 1, :] = right[m : m + 1, j * LANES : (j + 1) * LANES]
    for k in range(9):
        for j in range(8):
            vert[3 + k, j : j + 1, :] = precond[k : k + 1, j * LANES : (j + 1) * LANES]

    def precondition(vec):
        return [sum(vert[3 + 3 * m + l] * vec[l] for l in range(3)) for m in range(3)]

    ids[LIST_ROW : LIST_ROW + PEERS, :] = lists[:, 0, :]
    ids[LIST_ROW + PEERS : LIST_ROW + PEERS + 1, :] = jnp.concatenate([halo[1:2, :], halo[0:1, :]], axis=1)
    ids[LIST_ROW + PEERS + 1 : ID_ROWS, :] = jnp.zeros((ID_ROWS - LIST_ROW - PEERS - 1, LANES), jnp.int32)
    diag = lax.broadcasted_iota(jnp.int32, (16, PEERS), 0) == lax.broadcasted_iota(jnp.int32, (16, PEERS), 1)
    limit = jnp.sum(jnp.where(diag, jnp.broadcast_to(count[...], (16, PEERS)), 0).astype(F32), axis=1, keepdims=True)
    wide_row = lax.broadcasted_iota(jnp.int32, (16, LANES), 0)
    wide_lane = lax.broadcasted_iota(jnp.int32, (16, LANES), 1).astype(F32)
    list_live = jnp.where((wide_lane < limit) | (wide_row == HALO_ROW), 1.0, 0.0)

    def fill_own(vec):
        for m in range(3):
            for h in range(NODE_BLOCKS):
                own_tab[m, h] = spread(vec[m][h : h + 1, :])

    own_tables = [[own_tab.at[m, h] for h in range(NODE_BLOCKS)] for m in range(3)]
    got_tables = [[got_tab.at[m, k] for k in range(PEERS)] for m in range(3)]

    def read(tables):
        return [[t[...] for t in line] for line in tables]

    def offer(kept):
        got = [[], [], []]
        for g in range(2):
            found = pick(read(own_tables), ids[LIST_ROW + 8 * g : LIST_ROW + 8 * g + 8, :])
            for m in range(3):
                got[m].append(found[m] * list_live[8 * g : 8 * g + 8, :])
        for k in range(PEERS):
            for m in range(3):
                kept[k, m : m + 1, :] = got[m][k // 8][k % 8 : k % 8 + 1, :]
        for k in (UP, DOWN):
            for m in range(3):
                h = HALO_ROW
                kept[k, 3 + m : 4 + m, :] = got[m][h // 8][h % 8 : h % 8 + 1, :]

    def used(k, sign):
        return pl.ds(0, 6 if sign > 0 and k in (UP, DOWN) else 3)

    def exchange(src, dst, s_sem, r_sem, turn, sign, order=range(1, PEERS)):
        return [
            pltpu.make_async_remote_copy(
                src_ref=src.at[turn, k, used(k, sign)], dst_ref=dst.at[turn, k, used(k, sign)], send_sem=s_sem.at[turn, k],
                recv_sem=r_sem.at[turn, k], device_id=device(sign * OFFSETS[k]), device_id_type=MESH,
            )
            for k in order
        ]

    started = []

    def own_lookups():
        def elem_group(g, carry):
            rows = pl.ds(pl.multiple_of(g * 8, 8), 8)
            found = pick(read(own_tables), ids[rows, :])
            for m in range(3):
                zelem[m, rows, :] = found[m]
            return carry

        lax.fori_loop(0, 16, elem_group, 0)
        for g in range(2):
            found = pick(read(own_tables), ids[POINT_ROW + 8 * g : POINT_ROW + 8 * g + 8, :])
            for m in range(3):
                zpoint[m, 8 * g : 8 * g + 8, :] = found[m]

    def energy(first, last, z):
        low = z[0]
        for c in range(1, 8):
            low = jnp.where(row == c, z[c], low)
        high = jnp.zeros((8, LANES), F32)
        for c in range(4):
            high = jnp.where(row == c, z[8 + c], high)
        return first * low + last * high

    def element_products(turn):
        rim = [
            jnp.where(lane < 64, spread(recv_v[turn, UP, 3 + m : 4 + m, :]), spread(recv_v[turn, DOWN, 3 + m : 4 + m, :]))
            for m in range(3)
        ]
        power = jnp.zeros((8, LANES), F32)
        for pair in range(ELEM_CHUNKS // 2):
            here = ids[8 * pair : 8 * pair + 8, :]
            hit = (here >> 7) == NODE_BLOCKS
            z8 = []
            for m in range(3):
                value = jnp.take_along_axis(rim[m], here & 127, axis=1, mode="promise_in_bounds")
                z8.append(jnp.where(hit, value, zelem[m, 8 * pair : 8 * pair + 8, :]))
            for half in range(2):
                chunk = 2 * pair + half
                z = [spread(z8[m][half * 4 + a : half * 4 + a + 1, :]) for a in range(4) for m in range(3)]
                first, last = block_product(ehess, chunk * LANES, z, row)
                power = power + energy(first, last, z)
                for a, y8 in enumerate(vertex_rows(first, last, row)):
                    yelem[chunk * 4 + a] = y8
        return power

    def contact_products(turn):
        for k in range(PEERS):
            for m in range(3):
                got_tab[m, k] = spread(recv_v[turn, k, m : m + 1, :])

        power = jnp.zeros((8, LANES), F32)
        for c in range(PAIR_CHUNKS // 8):
            zp = [zpoint[m, 8 * c : 8 * c + 8, :] for m in range(3)]
            alive = live[8 * c : 8 * c + 8, :].astype(F32)
            first_slot = SLOT_ROW + 24 * c
            zs = [pick(read(got_tables), ids[first_slot + 8 * i : first_slot + 8 * i + 8, :]) for i in range(3)]
            for q in range(8):
                chunk = c * 8 + q
                z = [spread(zp[m][q : q + 1, :]) for m in range(3)]
                where = [(3 * q + a) for a in range(3)]
                z += [spread(zs[w // 8][m][w % 8 : w % 8 + 1, :]) for w in where for m in range(3)]
                first, last = block_product(chess, chunk * LANES, z, row)
                gate = spread(alive[q : q + 1, :])
                first, last = first * gate, last * gate
                power = power + energy(first, last, z)
                ys = vertex_rows(first, last, row)
                ypoint[chunk] = ys[0]
                for a in range(3):
                    yslot[chunk * 3 + a] = ys[1 + a]
        return power

    def scatter(held, base, blocks, rows):
        placed = []
        for u, y8 in enumerate(held):
            if u % 8 == 0:
                block8 = ids[base + u : base + u + 8, :] >> 7
            placed.append(place(y8, spread(block8[u % 8 : u % 8 + 1, :]), blocks, rows))
        k0, k1 = base * LANES, (base + len(held)) * LANES
        return gather_sum(jnp.concatenate(placed, axis=1), hot[k0:k1, :])

    def finish(turn, acc, vec):
        placed = []
        for k in range(PEERS + 1):
            if k < PEERS:
                got = recv_r[turn, k] * spread(list_live[k : k + 1, :])
            else:
                got = jnp.where(lane < 64, recv_h[turn, 0], recv_h[turn, 1])
            top, rest = split(got)
            y8 = jnp.where(row < 3, top, pltpu.roll(rest, 3, 0))
            placed.append(y8)
        back = scatter(placed, LIST_ROW, NODE_BLOCKS, 64)
        total[...] = acc[:64] + back
        return [
            mass[...] * vec[m] + (total[pl.ds(m, 8, stride=8), :] + total[pl.ds(m + 3, 8, stride=8), :])
            for m in range(3)
        ]

    def rows_of(values):
        out = jnp.zeros((8, LANES), F32)
        for i, value in enumerate(values):
            out = jnp.where(row == i, jnp.sum(value, axis=0, keepdims=True), out)
        return out

    def dot(a, b):
        return a[0] * b[0] + a[1] * b[1] + a[2] * b[2]

    def start_sub(turn, mine):
        sum_send[turn, 0] = mine
        out = [
            pltpu.make_async_remote_copy(
                src_ref=sum_send.at[turn, 0, pl.ds(0, 3)], dst_ref=sum_a.at[turn, j - 1, pl.ds(0, 3)], send_sem=ss_sem.at[turn, j - 1],
                recv_sem=ra_sem.at[turn, j - 1], device_id=sub_peer(j), device_id_type=MESH,
            )
            for j in range(1, 8)
        ]
        for copy in out:
            copy.start()
        return out

    def start_region(turn, first):
        for copy in first:
            copy.wait_recv()
        sum_send[turn, 1] = sum_send[turn, 0] + sum(sum_a[turn, j] for j in range(7))
        out = [
            pltpu.make_async_remote_copy(
                src_ref=sum_send.at[turn, 1, pl.ds(0, 3)], dst_ref=sum_b.at[turn, j - 1, pl.ds(0, 3)], send_sem=ss_sem.at[turn, 6 + j],
                recv_sem=rb_sem.at[turn, j - 1], device_id=region_peer(j), device_id_type=MESH,
            )
            for j in range(1, 16)
        ]
        for copy in out:
            copy.start()
        return out

    def end_sums(turn, second):
        for copy in second:
            copy.wait_recv()
        whole = sum_send[turn, 1] + sum(sum_b[turn, j] for j in range(15))
        whole = jnp.sum(whole, axis=1, keepdims=True)
        return [whole[i : i + 1, :] for i in range(3)]

    def operate(turn, vec, copies, early, late, sums):
        started.extend(copies)
        early()
        own_lookups()
        recv_v[turn, 0] = send_v[turn, 0]
        for k in (UP, DOWN):
            copies[k - 1].wait_recv()
        power = element_products(turn)
        for k in range(1, PEERS):
            if k not in (UP, DOWN):
                copies[k - 1].wait_recv()
        power = power + contact_products(turn)
        power = power + mass[...] * dot(vec, vec)
        sub_copies = start_sub(turn, rows_of([power] + sums))

        acc_slot = scatter([yslot[u] for u in range(3 * PAIR_CHUNKS)], SLOT_ROW, PEERS, 8 * PEERS)
        back = exchange(send_r, recv_r, sr_sem, rr_sem, turn, -1, FAR_FIRST)
        for i, k in enumerate(FAR_FIRST + (0,)):
            out = acc_slot[8 * k : 8 * k + 8]
            out = out + pltpu.roll(out, 5, 0)
            if k == 0:
                recv_r[turn, 0] = out
            else:
                send_r[turn, k] = out
                back[i].start()
        own_rows = [yelem[u] for u in range(4 * ELEM_CHUNKS)] + [ypoint[u] for u in range(PAIR_CHUNKS)]
        acc = scatter(own_rows, ELEM_ROW, 9, OWN_ROWS)
        rim = acc[64:72]
        send_h[turn] = rim + pltpu.roll(rim, 5, 0)
        rims = [
            pltpu.make_async_remote_copy(
                src_ref=send_h.at[turn, pl.ds(0, 3)], dst_ref=recv_h.at[turn, i, pl.ds(0, 3)], send_sem=sh_sem.at[turn, i],
                recv_sem=rh_sem.at[turn, i], device_id=device(-OFFSETS[k]), device_id_type=MESH,
            )
            for i, k in enumerate((UP, DOWN))
        ]
        for copy in rims:
            copy.start()
        late()
        region_copies = start_region(turn, sub_copies)
        started.extend(rims + back + sub_copies)
        if turn == 1:
            for copy in started:
                copy.wait_send()
        for copy in rims + back:
            copy.wait_recv()
        return finish(turn, acc, vec), region_copies

    rhs = [vert[m] for m in range(3)]
    d0 = precondition(rhs)
    fill_own(d0)
    offer(send_v.at[0])
    copies_v = exchange(send_v, recv_v, sv_sem, rv_sem, 0, 1)

    tall = lax.broadcasted_iota(jnp.int32, (LANES, LANES), 0)

    def hot_rows(first, last):
        def group(g, carry):
            low8 = ids[pl.ds(pl.multiple_of(g * 8, 8), 8), :] & 127
            for q in range(8):
                hit = jnp.broadcast_to(low8[q : q + 1, :], (LANES, LANES)) == tall
                k0 = pl.multiple_of((g * 8 + q) * LANES, LANES)
                hot[pl.ds(k0, LANES), :] = jnp.where(hit, 1.0, 0.0).astype(BF16).T
            return carry

        lax.fori_loop(first, last, group, 0)

    def prepare():
        for copy in copies[6:10]:
            copy.wait()
        for chunk in range(ELEM_CHUNKS):
            ids[4 * chunk : 4 * chunk + 4, :] = enodes[:, chunk * LANES : (chunk + 1) * LANES]
        ids[POINT_ROW : POINT_ROW + PAIR_CHUNKS, :] = point[...]
        for chunk in range(PAIR_CHUNKS):
            ids[SLOT_ROW + 3 * chunk : SLOT_ROW + 3 * chunk + 3, :] = slot[:, chunk * LANES : (chunk + 1) * LANES]

        hot_rows(0, LIST_ROW // 8)
        for copy in copies[10:]:
            copy.wait()

    pl.semaphore_wait(barrier, len(greeted))
    for copy in copies_v:
        copy.start()
    u0, region0 = operate(
        0, d0, copies_v, prepare, lambda: hot_rows(LIST_ROW // 8, ID_ROWS // 8), [dot(rhs, d0)]
    )

    largest = jnp.maximum(jnp.maximum(jnp.abs(u0[0]), jnp.abs(u0[1])), jnp.abs(u0[2]))
    largest = jnp.max(jnp.max(largest, axis=1, keepdims=True), axis=0, keepdims=True)
    largest = jnp.maximum(largest, 1e-30)
    unit = 1.0 / largest
    fill_own(precondition([u0[m] * unit for m in range(3)]))
    offer(step_v)
    curve0, gamma0, _ = end_sums(0, region0)
    alpha = gamma0 / curve0
    factor = spread(alpha * largest)
    copies_v = exchange(send_v, recv_v, sv_sem, rv_sem, 1, 1)
    for k in range(1, PEERS):
        send_v[1, k] = send_v[0, k] - factor * step_v[k]
        copies_v[k - 1].start()
    send_v[1, 0] = send_v[0, 0] - factor * step_v[0]
    r1 = [rhs[m] - alpha * u0[m] for m in range(3)]
    s1 = precondition(r1)
    fill_own(s1)
    a1, region1 = operate(1, s1, copies_v, lambda: None, lambda: None, [dot(r1, s1), dot(s1, u0)])
    for copy in region0 + region1:
        copy.wait_send()
    same, gamma1, cross = end_sums(1, region1)
    beta = gamma1 / gamma0
    curve1 = same + 2.0 * beta * cross + beta * beta * curve0
    alpha1 = gamma1 / curve1
    for m in range(3):
        d1 = s1[m] + beta * d0[m]
        image = a1[m] + beta * u0[m]
        out_s = alpha * d0[m] + alpha1 * d1
        out_r = r1[m] - alpha1 * image
        for j in range(8):
            out_ref[m : m + 1, j * LANES : (j + 1) * LANES] = out_s[j : j + 1, :]
            out_ref[3 + m : 4 + m, j * LANES : (j + 1) * LANES] = out_r[j : j + 1, :]


def per_device(
    right_side, node_mass, precond, elem_hess, elem_nodes, halo_lists, contact_hess, pair_point, pair_slot,
    pair_live, contact_send, send_counts,
):
    any_space = pl.BlockSpec(memory_space=pl.ANY)
    vmem = pl.BlockSpec(memory_space=pltpu.VMEM)
    args = (
        right_side, node_mass.reshape(8, LANES), precond, elem_hess, elem_nodes, halo_lists, contact_hess,
        pair_point.reshape(-1, LANES), pair_slot, pair_live.reshape(-1, LANES), contact_send.swapaxes(0, 1), send_counts,
    )
    out = jax.ShapeDtypeStruct((6, right_side.shape[1]), F32)
    dma = pltpu.SemaphoreType.DMA
    both = pl.pallas_call(
        kernel,
        out_shape=out,
        in_specs=[any_space] * len(args),
        out_specs=vmem,
        scratch_shapes=[pltpu.VMEM(a.shape, a.dtype) for a in args]
        + [
            pltpu.VMEM((ID_ROWS, LANES), jnp.int32),
            pltpu.VMEM((ID_ROWS * LANES, LANES), BF16),
            pltpu.VMEM((3, 8, LANES), F32),
            pltpu.VMEM((3, NODE_BLOCKS, 8, LANES), F32),
            pltpu.VMEM((3, PEERS, 8, LANES), F32),
            pltpu.VMEM((3, 4 * ELEM_CHUNKS, LANES), F32),
            pltpu.VMEM((3, PAIR_CHUNKS, LANES), F32),
            pltpu.VMEM((12, 8, LANES), F32),
            pltpu.VMEM((64, LANES), F32),
            pltpu.VMEM((4 * ELEM_CHUNKS, 8, LANES), F32),
            pltpu.VMEM((PAIR_CHUNKS, 8, LANES), F32),
            pltpu.VMEM((3 * PAIR_CHUNKS, 8, LANES), F32),
            pltpu.VMEM((2, PEERS, 8, LANES), F32),
            pltpu.VMEM((PEERS, 8, LANES), F32),
            pltpu.VMEM((2, PEERS, 8, LANES), F32),
            pltpu.VMEM((2, PEERS, 8, LANES), F32),
            pltpu.VMEM((2, PEERS, 8, LANES), F32),
            pltpu.VMEM((2, 8, LANES), F32),
            pltpu.VMEM((2, 2, 8, LANES), F32),
            pltpu.VMEM((2, 2, 8, LANES), F32),
            pltpu.VMEM((2, 7, 8, LANES), F32),
            pltpu.VMEM((2, 15, 8, LANES), F32),
            dma((len(args),)),
            dma((2, PEERS)),
            dma((2, PEERS)),
            dma((2, PEERS)),
            dma((2, PEERS)),
            dma((2, 2)),
            dma((2, 2)),
            dma((2, 22)),
            dma((2, 7)),
            dma((2, 15)),
        ],
        compiler_params=pltpu.CompilerParams(
            collective_id=0, has_side_effects=True, vmem_limit_bytes=60 * 1024 * 1024
        ),
    )(*args)
    return both[:3], both[3:]


def solution(mesh):
    both = P(None, AXES)
    return jax.shard_map(
        per_device,
        mesh=mesh,
        in_specs=(
            both, P(AXES), both, both, both, both, both, P(AXES), both, P(AXES), P(AXES, None, None), P(AXES, None),
        ),
        out_specs=(both, both),
        check_vma=False,
    )
```

```python
import jax
import jax.numpy as jnp
from jax import lax
from jax.experimental import pallas as pl
from jax.experimental.pallas import tpu as pltpu
from jax.sharding import PartitionSpec as P

MESH = pl.DeviceIdType.MESH
AXES = ("region", "sub")
F32 = jnp.float32
BF16 = jnp.bfloat16
LANES = 128
OFFSETS = (0, 1, 2, 3, 4, -1, -2, -3, -4, 64, 65, 63)
PEERS = len(OFFSETS)
UP, DOWN = 1, 5
NODE_BLOCKS = 8
ELEM_CHUNKS = 32
PAIR_CHUNKS = 16
ELEM_ROW, POINT_ROW, SLOT_ROW, LIST_ROW, ID_ROWS = 0, 128, 144, 192, 208
HALO_ROW = PEERS
OWN_ROWS = 80


def spread(row):
    return jnp.broadcast_to(row, (8, LANES))


def pick(tables, ids):
    block, lane = ids >> 7, ids & 127
    found = [jnp.zeros(ids.shape, F32) for _ in range(3)]
    for h in range(len(tables[0])):
        hit = block == h
        for m in range(3):
            value = jnp.take_along_axis(tables[m][h], lane, axis=1, mode="promise_in_bounds")
            found[m] = jnp.where(hit, value, found[m])
    return found


def block_product(hess, start, z, row):
    lanes = pl.ds(start, LANES)
    low = row < 4
    acc0 = acc1 = acc2 = None
    for j in range(6):
        za, zb = z[2 * j], z[2 * j + 1]
        t0 = hess[24 * j : 24 * j + 8, lanes] * za
        t1 = hess[24 * j + 8 : 24 * j + 16, lanes] * jnp.where(low, za, zb)
        t2 = hess[24 * j + 16 : 24 * j + 24, lanes] * zb
        if j == 0:
            acc0, acc1, acc2 = t0, t1, t2
        else:
            acc0, acc1, acc2 = acc0 + t0, acc1 + t1, acc2 + t2
    first = acc0 + pltpu.roll(jnp.where(low, acc2, acc1), 4, 0)
    last = acc1 + pltpu.roll(acc2, 4, 0)
    return first, last


def split(x):
    top = x.astype(BF16).astype(F32)
    return top, x - top


def vertex_rows(first, last, row):
    f0, f1 = split(first)
    l0, l1 = split(last)
    near = row < 3
    a0 = jnp.where(near, f0, pltpu.roll(f1, 3, 0))
    a1 = jnp.where(near, pltpu.roll(f0, 5, 0), f1)
    fl0 = jnp.where(row < 1, l0, f0)
    fl1 = jnp.where(row < 1, l1, f1)
    a2 = jnp.where(near, pltpu.roll(fl0, 2, 0), pltpu.roll(fl1, 5, 0))
    a3 = jnp.where(near, pltpu.roll(l0, 7, 0), pltpu.roll(l1, 2, 0))
    return a0, a1, a2, a3


def place(y8, block, count, rows):
    parts = [jnp.where(block == h, y8, 0.0) for h in range(count)]
    if rows > 8 * count:
        parts.append(jnp.zeros((rows - 8 * count, LANES), F32))
    return jnp.concatenate(parts, axis=0).astype(BF16)


def gather_sum(placed, hot):
    return jnp.dot(placed, hot, preferred_element_type=F32)


def kernel(
    right_hbm, mass_hbm, precond_hbm, ehess_hbm, enodes_hbm, halo_hbm, chess_hbm, point_hbm, slot_hbm,
    live_hbm, list_hbm, count_hbm,
    out_ref,
    right, mass, precond, ehess, enodes, halo, chess, point, slot, live, lists, count,
    ids, hot, ztab, own_tab, got_tab, zelem, zpoint, vert, total,
    yelem, ypoint, yslot, send_v, step_v, recv_v, send_r, recv_r, send_h, recv_h, sum_send, sum_a, sum_b,
    in_sem, sv_sem, rv_sem, sr_sem, rr_sem, sh_sem, rh_sem, ss_sem, ra_sem, rb_sem,
):
    region, sub = lax.axis_index("region"), lax.axis_index("sub")
    part = region * 8 + sub

    known = {}

    def device(offset):
        offset %= 128
        if offset not in known:
            q = lax.rem(part + offset, 128)
            known[offset] = (lax.div(q, 8), lax.rem(q, 8))
        return known[offset]

    def sub_peer(j):
        return (region, lax.rem(sub + j, 8))

    def region_peer(j):
        return (lax.rem(region + j, 16), sub)

    barrier = pltpu.get_barrier_semaphore()
    greeted = [device(o) for o in OFFSETS[1:]] + [sub_peer(j) for j in range(1, 8)]
    greeted += [region_peer(j) for j in range(1, 16) if j != 8]
    for peer in greeted:
        pl.semaphore_signal(barrier, inc=1, device_id=peer, device_id_type=MESH)

    pairs = [
        (right_hbm, right), (precond_hbm, precond), (list_hbm, lists), (count_hbm, count), (halo_hbm, halo),
        (mass_hbm, mass), (enodes_hbm, enodes), (point_hbm, point), (slot_hbm, slot), (live_hbm, live),
        (chess_hbm, chess), (ehess_hbm, ehess),
    ]
    copies = [pltpu.make_async_copy(src, dst, in_sem.at[i]) for i, (src, dst) in enumerate(pairs)]
    for copy in copies:
        copy.start()

    row = lax.broadcasted_iota(jnp.int32, (8, LANES), 0)
    lane = lax.broadcasted_iota(jnp.int32, (8, LANES), 1)

    for copy in copies[:6]:
        copy.wait()
    for m in range(3):
        for j in range(8):
            vert[m, j : j + 1, :] = right[m : m + 1, j * LANES : (j + 1) * LANES]
    for k in range(9):
        for j in range(8):
            vert[3 + k, j : j + 1, :] = precond[k : k + 1, j * LANES : (j + 1) * LANES]

    def precondition(vec):
        return [sum(vert[3 + 3 * m + l] * vec[l] for l in range(3)) for m in range(3)]

    ids[LIST_ROW : LIST_ROW + PEERS, :] = lists[:, 0, :]
    ids[LIST_ROW + PEERS : LIST_ROW + PEERS + 1, :] = jnp.concatenate([halo[1:2, :], halo[0:1, :]], axis=1)
    ids[LIST_ROW + PEERS + 1 : ID_ROWS, :] = jnp.zeros((ID_ROWS - LIST_ROW - PEERS - 1, LANES), jnp.int32)
    diag = lax.broadcasted_iota(jnp.int32, (16, PEERS), 0) == lax.broadcasted_iota(jnp.int32, (16, PEERS), 1)
    limit = jnp.sum(jnp.where(diag, jnp.broadcast_to(count[...], (16, PEERS)), 0).astype(F32), axis=1, keepdims=True)
    wide_row = lax.broadcasted_iota(jnp.int32, (16, LANES), 0)
    wide_lane = lax.broadcasted_iota(jnp.int32, (16, LANES), 1).astype(F32)
    list_live = jnp.where((wide_lane < limit) | (wide_row == HALO_ROW), 1.0, 0.0)

    def fill_own(vec):
        for m in range(3):
            for h in range(NODE_BLOCKS):
                own_tab[m, h] = spread(vec[m][h : h + 1, :])

    own_tables = [[own_tab.at[m, h] for h in range(NODE_BLOCKS)] for m in range(3)]
    got_tables = [[got_tab.at[m, k] for k in range(PEERS)] for m in range(3)]

    def read(tables):
        return [[t[...] for t in line] for line in tables]

    def offer(kept):
        got = [[], [], []]
        for g in range(2):
            found = pick(read(own_tables), ids[LIST_ROW + 8 * g : LIST_ROW + 8 * g + 8, :])
            for m in range(3):
                got[m].append(found[m] * list_live[8 * g : 8 * g + 8, :])
        for k in range(PEERS):
            for m in range(3):
                kept[k, m : m + 1, :] = got[m][k // 8][k % 8 : k % 8 + 1, :]
        for k in (UP, DOWN):
            for m in range(3):
                h = HALO_ROW
                kept[k, 3 + m : 4 + m, :] = got[m][h // 8][h % 8 : h % 8 + 1, :]

    def used(k, sign):
        return pl.ds(0, 6 if sign > 0 and k in (UP, DOWN) else 3)

    def exchange(src, dst, s_sem, r_sem, turn, sign):
        return [
            pltpu.make_async_remote_copy(
                src_ref=src.at[turn, k, used(k, sign)], dst_ref=dst.at[turn, k, used(k, sign)], send_sem=s_sem.at[turn, k],
                recv_sem=r_sem.at[turn, k], device_id=device(sign * OFFSETS[k]), device_id_type=MESH,
            )
            for k in range(1, PEERS)
        ]

    started = []

    def own_lookups():
        def elem_group(g, carry):
            rows = pl.ds(pl.multiple_of(g * 8, 8), 8)
            found = pick(read(own_tables), ids[rows, :])
            for m in range(3):
                zelem[m, rows, :] = found[m]
            return carry

        lax.fori_loop(0, 16, elem_group, 0)
        for g in range(2):
            found = pick(read(own_tables), ids[POINT_ROW + 8 * g : POINT_ROW + 8 * g + 8, :])
            for m in range(3):
                zpoint[m, 8 * g : 8 * g + 8, :] = found[m]

    def energy(first, last, z):
        low = z[0]
        for c in range(1, 8):
            low = jnp.where(row == c, z[c], low)
        high = jnp.zeros((8, LANES), F32)
        for c in range(4):
            high = jnp.where(row == c, z[8 + c], high)
        return first * low + last * high

    def element_products(turn):
        rim = [
            jnp.where(lane < 64, spread(recv_v[turn, UP, 3 + m : 4 + m, :]), spread(recv_v[turn, DOWN, 3 + m : 4 + m, :]))
            for m in range(3)
        ]
        power = jnp.zeros((8, LANES), F32)
        for pair in range(ELEM_CHUNKS // 2):
            here = ids[8 * pair : 8 * pair + 8, :]
            hit = (here >> 7) == NODE_BLOCKS
            z8 = []
            for m in range(3):
                value = jnp.take_along_axis(rim[m], here & 127, axis=1, mode="promise_in_bounds")
                z8.append(jnp.where(hit, value, zelem[m, 8 * pair : 8 * pair + 8, :]))
            for half in range(2):
                chunk = 2 * pair + half
                z = [spread(z8[m][half * 4 + a : half * 4 + a + 1, :]) for a in range(4) for m in range(3)]
                first, last = block_product(ehess, chunk * LANES, z, row)
                power = power + energy(first, last, z)
                for a, y8 in enumerate(vertex_rows(first, last, row)):
                    yelem[chunk * 4 + a] = y8
        return power

    def contact_products(turn):
        for k in range(PEERS):
            for m in range(3):
                got_tab[m, k] = spread(recv_v[turn, k, m : m + 1, :])

        power = jnp.zeros((8, LANES), F32)
        for c in range(PAIR_CHUNKS // 8):
            zp = [zpoint[m, 8 * c : 8 * c + 8, :] for m in range(3)]
            alive = live[8 * c : 8 * c + 8, :].astype(F32)
            first_slot = SLOT_ROW + 24 * c
            zs = [pick(read(got_tables), ids[first_slot + 8 * i : first_slot + 8 * i + 8, :]) for i in range(3)]
            for q in range(8):
                chunk = c * 8 + q
                z = [spread(zp[m][q : q + 1, :]) for m in range(3)]
                where = [(3 * q + a) for a in range(3)]
                z += [spread(zs[w // 8][m][w % 8 : w % 8 + 1, :]) for w in where for m in range(3)]
                first, last = block_product(chess, chunk * LANES, z, row)
                gate = spread(alive[q : q + 1, :])
                first, last = first * gate, last * gate
                power = power + energy(first, last, z)
                ys = vertex_rows(first, last, row)
                ypoint[chunk] = ys[0]
                for a in range(3):
                    yslot[chunk * 3 + a] = ys[1 + a]
        return power

    def scatter(held, base, blocks, rows):
        placed = []
        for u, y8 in enumerate(held):
            if u % 8 == 0:
                block8 = ids[base + u : base + u + 8, :] >> 7
            placed.append(place(y8, spread(block8[u % 8 : u % 8 + 1, :]), blocks, rows))
        k0, k1 = base * LANES, (base + len(held)) * LANES
        return gather_sum(jnp.concatenate(placed, axis=1), hot[k0:k1, :])

    def finish(turn, acc, vec):
        placed = []
        for k in range(PEERS + 1):
            if k < PEERS:
                got = recv_r[turn, k] * spread(list_live[k : k + 1, :])
            else:
                got = jnp.where(lane < 64, recv_h[turn, 0], recv_h[turn, 1])
            top, rest = split(got)
            y8 = jnp.where(row < 3, top, pltpu.roll(rest, 3, 0))
            placed.append(y8)
        back = scatter(placed, LIST_ROW, NODE_BLOCKS, 64)
        total[...] = acc[:64] + back
        return [
            mass[...] * vec[m] + (total[pl.ds(m, 8, stride=8), :] + total[pl.ds(m + 3, 8, stride=8), :])
            for m in range(3)
        ]

    def rows_of(values):
        out = jnp.zeros((8, LANES), F32)
        for i, value in enumerate(values):
            out = jnp.where(row == i, jnp.sum(value, axis=0, keepdims=True), out)
        return out

    def dot(a, b):
        return a[0] * b[0] + a[1] * b[1] + a[2] * b[2]

    def start_sub(turn, mine):
        sum_send[turn, 0] = mine
        out = [
            pltpu.make_async_remote_copy(
                src_ref=sum_send.at[turn, 0, pl.ds(0, 3)], dst_ref=sum_a.at[turn, j - 1, pl.ds(0, 3)], send_sem=ss_sem.at[turn, j - 1],
                recv_sem=ra_sem.at[turn, j - 1], device_id=sub_peer(j), device_id_type=MESH,
            )
            for j in range(1, 8)
        ]
        for copy in out:
            copy.start()
        return out

    def start_region(turn, first):
        for copy in first:
            copy.wait_recv()
        sum_send[turn, 1] = sum_send[turn, 0] + sum(sum_a[turn, j] for j in range(7))
        out = [
            pltpu.make_async_remote_copy(
                src_ref=sum_send.at[turn, 1, pl.ds(0, 3)], dst_ref=sum_b.at[turn, j - 1, pl.ds(0, 3)], send_sem=ss_sem.at[turn, 6 + j],
                recv_sem=rb_sem.at[turn, j - 1], device_id=region_peer(j), device_id_type=MESH,
            )
            for j in range(1, 16)
        ]
        for copy in out:
            copy.start()
        return out

    def end_sums(turn, second):
        for copy in second:
            copy.wait_recv()
        whole = sum_send[turn, 1] + sum(sum_b[turn, j] for j in range(15))
        whole = jnp.sum(whole, axis=1, keepdims=True)
        return [whole[i : i + 1, :] for i in range(3)]

    def operate(turn, vec, copies, early, late, sums):
        started.extend(copies)
        early()
        own_lookups()
        recv_v[turn, 0] = send_v[turn, 0]
        for k in (UP, DOWN):
            copies[k - 1].wait_recv()
        power = element_products(turn)
        for k in range(1, PEERS):
            if k not in (UP, DOWN):
                copies[k - 1].wait_recv()
        power = power + contact_products(turn)
        power = power + mass[...] * dot(vec, vec)
        sub_copies = start_sub(turn, rows_of([power] + sums))

        acc_slot = scatter([yslot[u] for u in range(3 * PAIR_CHUNKS)], SLOT_ROW, PEERS, 8 * PEERS)
        for k in range(PEERS):
            out = acc_slot[8 * k : 8 * k + 8]
            out = out + pltpu.roll(out, 5, 0)
            if k == 0:
                recv_r[turn, 0] = out
            else:
                send_r[turn, k] = out
        back = exchange(send_r, recv_r, sr_sem, rr_sem, turn, -1)
        for copy in back:
            copy.start()
        own_rows = [yelem[u] for u in range(4 * ELEM_CHUNKS)] + [ypoint[u] for u in range(PAIR_CHUNKS)]
        acc = scatter(own_rows, ELEM_ROW, 9, OWN_ROWS)
        rim = acc[64:72]
        send_h[turn] = rim + pltpu.roll(rim, 5, 0)
        rims = [
            pltpu.make_async_remote_copy(
                src_ref=send_h.at[turn, pl.ds(0, 3)], dst_ref=recv_h.at[turn, i, pl.ds(0, 3)], send_sem=sh_sem.at[turn, i],
                recv_sem=rh_sem.at[turn, i], device_id=device(-OFFSETS[k]), device_id_type=MESH,
            )
            for i, k in enumerate((UP, DOWN))
        ]
        for copy in rims:
            copy.start()
        late()
        region_copies = start_region(turn, sub_copies)
        started.extend(rims + back + sub_copies)
        if turn == 1:
            for copy in started:
                copy.wait_send()
        for copy in rims + back:
            copy.wait_recv()
        return finish(turn, acc, vec), region_copies

    rhs = [vert[m] for m in range(3)]
    d0 = precondition(rhs)
    fill_own(d0)
    offer(send_v.at[0])
    copies_v = exchange(send_v, recv_v, sv_sem, rv_sem, 0, 1)

    tall = lax.broadcasted_iota(jnp.int32, (LANES, LANES), 0)

    def hot_rows(first, last):
        def group(g, carry):
            low8 = ids[pl.ds(pl.multiple_of(g * 8, 8), 8), :] & 127
            for q in range(8):
                hit = jnp.broadcast_to(low8[q : q + 1, :], (LANES, LANES)) == tall
                k0 = pl.multiple_of((g * 8 + q) * LANES, LANES)
                hot[pl.ds(k0, LANES), :] = jnp.where(hit, 1.0, 0.0).astype(BF16).T
            return carry

        lax.fori_loop(first, last, group, 0)

    def prepare():
        for copy in copies[6:10]:
            copy.wait()
        for chunk in range(ELEM_CHUNKS):
            ids[4 * chunk : 4 * chunk + 4, :] = enodes[:, chunk * LANES : (chunk + 1) * LANES]
        ids[POINT_ROW : POINT_ROW + PAIR_CHUNKS, :] = point[...]
        for chunk in range(PAIR_CHUNKS):
            ids[SLOT_ROW + 3 * chunk : SLOT_ROW + 3 * chunk + 3, :] = slot[:, chunk * LANES : (chunk + 1) * LANES]

        hot_rows(0, LIST_ROW // 8)
        for copy in copies[10:]:
            copy.wait()

    pl.semaphore_wait(barrier, len(greeted))
    for copy in copies_v:
        copy.start()
    u0, region0 = operate(
        0, d0, copies_v, prepare, lambda: hot_rows(LIST_ROW // 8, ID_ROWS // 8), [dot(rhs, d0)]
    )

    largest = jnp.maximum(jnp.maximum(jnp.abs(u0[0]), jnp.abs(u0[1])), jnp.abs(u0[2]))
    largest = jnp.max(jnp.max(largest, axis=1, keepdims=True), axis=0, keepdims=True)
    largest = jnp.maximum(largest, 1e-30)
    unit = 1.0 / largest
    fill_own(precondition([u0[m] * unit for m in range(3)]))
    offer(step_v)
    curve0, gamma0, _ = end_sums(0, region0)
    alpha = gamma0 / curve0
    factor = spread(alpha * largest)
    copies_v = exchange(send_v, recv_v, sv_sem, rv_sem, 1, 1)
    for k in range(1, PEERS):
        send_v[1, k] = send_v[0, k] - factor * step_v[k]
        copies_v[k - 1].start()
    send_v[1, 0] = send_v[0, 0] - factor * step_v[0]
    r1 = [rhs[m] - alpha * u0[m] for m in range(3)]
    s1 = precondition(r1)
    fill_own(s1)
    a1, region1 = operate(1, s1, copies_v, lambda: None, lambda: None, [dot(r1, s1), dot(s1, u0)])
    for copy in region0 + region1:
        copy.wait_send()
    same, gamma1, cross = end_sums(1, region1)
    beta = gamma1 / gamma0
    curve1 = same + 2.0 * beta * cross + beta * beta * curve0
    alpha1 = gamma1 / curve1
    for m in range(3):
        d1 = s1[m] + beta * d0[m]
        image = a1[m] + beta * u0[m]
        out_s = alpha * d0[m] + alpha1 * d1
        out_r = r1[m] - alpha1 * image
        for j in range(8):
            out_ref[m : m + 1, j * LANES : (j + 1) * LANES] = out_s[j : j + 1, :]
            out_ref[m : m + 1, (8 + j) * LANES : (9 + j) * LANES] = out_r[j : j + 1, :]


def per_device(
    right_side, node_mass, precond, elem_hess, elem_nodes, halo_lists, contact_hess, pair_point, pair_slot,
    pair_live, contact_send, send_counts,
):
    any_space = pl.BlockSpec(memory_space=pl.ANY)
    vmem = pl.BlockSpec(memory_space=pltpu.VMEM)
    args = (
        right_side, node_mass.reshape(8, LANES), precond, elem_hess, elem_nodes, halo_lists, contact_hess,
        pair_point.reshape(-1, LANES), pair_slot, pair_live.reshape(-1, LANES), contact_send.swapaxes(0, 1), send_counts,
    )
    out = jax.ShapeDtypeStruct((3, 2 * right_side.shape[1]), F32)
    dma = pltpu.SemaphoreType.DMA
    both = pl.pallas_call(
        kernel,
        out_shape=out,
        in_specs=[any_space] * len(args),
        out_specs=vmem,
        scratch_shapes=[pltpu.VMEM(a.shape, a.dtype) for a in args]
        + [
            pltpu.VMEM((ID_ROWS, LANES), jnp.int32),
            pltpu.VMEM((ID_ROWS * LANES, LANES), BF16),
            pltpu.VMEM((3, 8, LANES), F32),
            pltpu.VMEM((3, NODE_BLOCKS, 8, LANES), F32),
            pltpu.VMEM((3, PEERS, 8, LANES), F32),
            pltpu.VMEM((3, 4 * ELEM_CHUNKS, LANES), F32),
            pltpu.VMEM((3, PAIR_CHUNKS, LANES), F32),
            pltpu.VMEM((12, 8, LANES), F32),
            pltpu.VMEM((64, LANES), F32),
            pltpu.VMEM((4 * ELEM_CHUNKS, 8, LANES), F32),
            pltpu.VMEM((PAIR_CHUNKS, 8, LANES), F32),
            pltpu.VMEM((3 * PAIR_CHUNKS, 8, LANES), F32),
            pltpu.VMEM((2, PEERS, 8, LANES), F32),
            pltpu.VMEM((PEERS, 8, LANES), F32),
            pltpu.VMEM((2, PEERS, 8, LANES), F32),
            pltpu.VMEM((2, PEERS, 8, LANES), F32),
            pltpu.VMEM((2, PEERS, 8, LANES), F32),
            pltpu.VMEM((2, 8, LANES), F32),
            pltpu.VMEM((2, 2, 8, LANES), F32),
            pltpu.VMEM((2, 2, 8, LANES), F32),
            pltpu.VMEM((2, 7, 8, LANES), F32),
            pltpu.VMEM((2, 15, 8, LANES), F32),
            dma((len(args),)),
            dma((2, PEERS)),
            dma((2, PEERS)),
            dma((2, PEERS)),
            dma((2, PEERS)),
            dma((2, 2)),
            dma((2, 2)),
            dma((2, 22)),
            dma((2, 7)),
            dma((2, 15)),
        ],
        compiler_params=pltpu.CompilerParams(
            collective_id=0, has_side_effects=True, vmem_limit_bytes=60 * 1024 * 1024
        ),
    )(*args)
    own = right_side.shape[1]
    return both[:, :own], both[:, own:]


def solution(mesh):
    both = P(None, AXES)
    return jax.shard_map(
        per_device,
        mesh=mesh,
        in_specs=(
            both, P(AXES), both, both, both, both, both, P(AXES), both, P(AXES), P(AXES, None, None), P(AXES, None),
        ),
        out_specs=(both, both),
        check_vma=False,
    )
```
